256 devices in a mesh: depth: 8 (over x_lo, y), row: 16 (over z, x_hi), col: 2 (over core).
Axes of the slice: x: 4 (x_hi: 2, x_lo: 2; x = x_hi * 2 + x_lo), y: 4, z: 8, core: 2. Of those that a mesh axis runs over, the one named last changes fastest.
Arguments:
- phase: float32 [4096, 4096], P(('row', 'col')), may hold values from -3.140625 to 3.140625
- depths: int32 [8], P('depth'), may hold values from 0 to 63
- targets: float32 [8, 4096, 4096], P('depth', ('row', 'col')), may hold values from 0.1 to 3
Outputs:
- gradient: float32 [4096, 4096], P(('row', 'col'))
The draws below stay inside these ranges and needn't reach their ends.
All inputs are finite; a program needn't handle non-finite values.
Results may differ from the reference program's by a relative error of at most 0.0003.
Values sent between devices are 32-bit elements; how exact they have to be, the bound alone decides.
No kernel may reach another device: no remote copies, remote signals or barrier semaphores. Data moves between devices by JAX's collectives and lax.ppermute only.
A program may use at most 128 MiB of HBM per device.

```python
import math
import jax
import jax.numpy as jnp
from jax import lax

N = 4096
PLANES = 8


def with_ends(drawn, key, least, top_value):
    spot = [jax.random.randint(jax.random.fold_in(key, axis), (), 0, length) for axis, length in enumerate(drawn.shape)]
    main_axis = drawn.shape.index(max(drawn.shape))
    neighbour = spot[:main_axis] + [(spot[main_axis] + 1) % drawn.shape[main_axis]] + spot[main_axis + 1:]
    return drawn.at[tuple(spot)].set(least).at[tuple(neighbour)].set(top_value)


def level_of(stream_key, shape, split, least, largest):
    def one(dim, blocks):
        steps = jax.random.uniform(jax.random.fold_in(jax.random.fold_in(stream_key, 6), dim), (blocks,), jnp.float32, least / len(split), largest / len(split))
        return jnp.repeat(jnp.exp(steps), shape[dim] // blocks).reshape((-1,) + (1,) * (len(shape) - dim - 1))

    factor_of = one(*split[0])
    for cut in split[1:]:
        factor_of = factor_of * one(*cut)
    return factor_of


def setup_inputs(seed: int = 0) -> dict:
    arg_keys = jax.random.split(jax.random.key(seed), 4)
    phase = jnp.clip(jax.random.uniform(arg_keys[0], (N, N), jnp.float32, -3.140625, 3.140625), -3.140625, 3.140625)
    depths = with_ends(jax.random.randint(arg_keys[1], (PLANES,), 0, 64), jax.random.fold_in(arg_keys[1], 1), 0, 63).astype(jnp.int32)
    targets = jnp.clip(jnp.exp(math.log(3.0) - 3.4011974 * jax.random.uniform(arg_keys[2], (PLANES, N, N), jnp.float32) ** level_of(arg_keys[2], (PLANES, N, N), ((0, 8), (1, 32)), -0.2, 0.2)), 0.1, 3.0)
    return dict(phase=phase, depths=depths, targets=targets)


def transfer(depth_value):
    counter = jnp.arange(N, dtype=jnp.int32)
    centered = jnp.where(counter < N // 2, counter, counter - N)
    squares = (centered * centered) % (2 * N)
    summed = (squares[:, None] + squares[None, :]) % (2 * N)
    strength = ((depth_value + 8) * (N // 64) + 1) % (2 * N)
    turned = ((strength * summed) % (2 * N)).astype(jnp.float32) * (-math.pi / N)
    return lax.complex(jnp.cos(turned), jnp.sin(turned))


def reference(phase, depths, targets):
    hologram = lax.complex(jnp.cos(phase), jnp.sin(phase))
    spectrum = jnp.fft.fft2(hologram)

    def one_plane(summed, plane_index):
        kernel = transfer(depths[plane_index])
        field = jnp.fft.ifft2(spectrum * kernel)
        intensity = jnp.real(field) ** 2 + jnp.imag(field) ** 2
        residual = (4.0 / PLANES) * (intensity - targets[plane_index])
        returned = jnp.conj(kernel) * jnp.fft.fft2(residual * field)
        return summed + returned, None

    adjoint, unused = lax.scan(one_plane, jnp.zeros_like(spectrum), jnp.arange(PLANES, dtype=jnp.int32))
    back = jnp.fft.ifft2(adjoint)
    return jnp.imag(back) * jnp.cos(phase) - jnp.real(back) * jnp.sin(phase)
```

```python
import math

import jax
import jax.numpy as jnp
import numpy as np
from jax import lax
from jax.experimental import pallas as pl
from jax.experimental.pallas import tpu as pltpu
from jax.sharding import Mesh
from jax.sharding import PartitionSpec as P

SLAB = ("xl", "y", "xh", "c")
OUTER = 32
INNER = 128
BLOCK = 16
F32 = jnp.float32
BF16 = jnp.bfloat16


def fit(function, count, odd):
    points = np.cos(np.pi * (np.arange(400) + 0.5) / 400) * 0.5
    powers = np.stack([points ** (2 * k + odd) for k in range(count)], axis=1)
    return [float(c) for c in np.linalg.lstsq(powers, function(np.pi * points), rcond=None)[0]]


SIN_TERMS = fit(np.sin, 6, 1)
COS_TERMS = fit(np.cos, 6, 0)


def horner(terms, square):
    total = jnp.full_like(square, terms[-1])
    for term in terms[-2::-1]:
        total = total * square + term
    return total


def unit_wave(turns):
    turns = turns - jnp.round(turns)
    square = turns * turns
    half_sin = turns * horner(SIN_TERMS, square)
    half_cos = horner(COS_TERMS, square)
    twice = half_sin + half_sin
    return 1.0 - twice * half_sin, twice * half_cos


def spin(value, step, size, sign):
    real, imag = value
    step = step % size
    if step == 0:
        return value
    if 4 * step == size:
        return (-imag, real) if sign > 0 else (imag, -real)
    if 2 * step == size:
        return (-real, -imag)
    if 4 * step == 3 * size:
        return (imag, -real) if sign > 0 else (-imag, real)
    cos = math.cos(2 * math.pi * step / size)
    sin = sign * math.sin(2 * math.pi * step / size)
    if 8 * step % size == 0 and abs(abs(cos) - abs(sin)) < 1e-9:
        root = abs(cos)
        real, imag = real * root, imag * root
        cs = 1 if cos > 0 else -1
        ss = 1 if sin > 0 else -1
        a = real if cs > 0 else -real
        new_real = a - imag if ss > 0 else a + imag
        b = imag if cs > 0 else -imag
        new_imag = b + real if ss > 0 else b - real
        return new_real, new_imag
    return real * cos - imag * sin, real * sin + imag * cos


def small_dft(values, sign):
    size = len(values)
    if size == 1:
        return values
    even = small_dft(values[0::2], sign)
    odd = small_dft(values[1::2], sign)
    low, high = [], []
    for k in range(size // 2):
        turned = spin(odd[k], k, size, sign)
        low.append((even[k][0] + turned[0], even[k][1] + turned[1]))
        high.append((even[k][0] - turned[0], even[k][1] - turned[1]))
    return low + high


def dft32(load, store, mid_ref, sign):
    for b in range(8):
        out = small_dft([load(8 * a + b) for a in range(4)], sign)
        for p in range(4):
            real, imag = spin(out[p], b * p, 32, sign)
            mid_ref[8 * p + b, 0] = real
            mid_ref[8 * p + b, 1] = imag
    for p in range(4):
        out = small_dft([(mid_ref[8 * p + b, 0], mid_ref[8 * p + b, 1]) for b in range(8)], sign)
        for s in range(8):
            store(p + 4 * s, out[s])


def split(value):
    high = value.astype(BF16)
    return high, (value - high.astype(F32)).astype(BF16)


def dot(left, right):
    return jnp.dot(left, right, preferred_element_type=F32)


def row_block(step):
    return pl.ds(pl.multiple_of(step * BLOCK, BLOCK), BLOCK)


def tile(index):
    return slice(index * INNER, (index + 1) * INNER)


def sort_kernel(target_ref, out_ref, turned_ref):
    for k in range(OUTER):
        turned_ref[tile(k), :] = target_ref[:, tile(k)].T
    for j in range(OUTER):
        out_ref[j] = turned_ref[pl.ds(j, INNER, stride=OUTER), :].T


def rows_kernel(phase_ref, row_ref, col_ref, tw_ref, dft_ref, out_ref, wave_ref, high_ref, low_ref, mid_ref, sh_ref, sl_ref):
    high_ref[...], low_ref[...] = split(dft_ref[...])

    def block(step, carry):
        rows = row_block(step)
        row_turn = row_ref[rows, :]

        def load(k):
            turns = phase_ref[rows, tile(k)] * (0.5 / math.pi) + (row_turn + col_ref[:, tile(k)])
            cos, sin = unit_wave(turns)
            wave_ref[0, rows, tile(k)] = cos
            wave_ref[1, rows, tile(k)] = sin
            return cos, sin

        def store(k, value):
            cos, sin = tw_ref[0, k : k + 1, :], tw_ref[1, k : k + 1, :]
            real, imag = value
            for part, side in ((real * cos - imag * sin, 0), (real * sin + imag * cos, 1)):
                high, low = split(part)
                sh_ref[k, rows, tile(side)] = high
                sl_ref[k, rows, tile(side)] = low

        dft32(load, store, mid_ref, -1)
        return carry

    lax.fori_loop(0, INNER // BLOCK, block, 0)

    def multiply(step, carry):
        group = pl.ds(step * 4, 4)
        high = sh_ref[group].reshape(4 * INNER, 2 * INNER)
        low = sl_ref[group].reshape(4 * INNER, 2 * INNER)
        out = dot(high, high_ref[...]) + dot(low, high_ref[...]) + dot(high, low_ref[...])
        out = out.reshape(4, INNER, 2 * INNER)
        out_ref[group, 0] = out[:, :, :INNER]
        out_ref[group, 1] = out[:, :, INNER:]
        return carry

    lax.fori_loop(0, OUTER // 4, multiply, 0)


def columns_kernel(
    scale, in_ref, target_ref, tw_ref, there_ref, home_ref, out_ref,
    fh_ref, fl_ref, bh_ref, bl_ref, mid_ref, sh_ref, sl_ref, back_ref,
):
    fh_ref[...], fl_ref[...] = split(home_ref[...])
    bh_ref[...], bl_ref[...] = split(there_ref[...])

    def forward(step, carry):
        rows = row_block(step)

        def load(k):
            return tuple(in_ref[step * 4 + k % 4, side, tile_rows(k // 4), :] for side in (0, 1))

        def store(k, value):
            cos, sin = tw_ref[0, k, rows, :], tw_ref[1, k, rows, :]
            real, imag = value
            for part, side in ((real * cos - imag * sin, 0), (real * sin + imag * cos, 1)):
                high, low = split(part)
                sh_ref[k, side, rows, :] = high
                sl_ref[k, side, rows, :] = low

        dft32(load, store, mid_ref, -1)
        return carry

    lax.fori_loop(0, INNER // BLOCK, forward, 0)

    def pair(ref, first):
        return jnp.concatenate([ref[first + k].reshape(2 * INNER, INNER) for k in (0, 1)], axis=1)

    def multiply(step, carry):
        first = step * 2
        high, low = pair(sh_ref, first), pair(sl_ref, first)
        field = dot(fh_ref[...], high) + dot(fh_ref[...], low) + dot(fl_ref[...], high)
        real, imag = field[:INNER], field[INNER:]
        target = jnp.concatenate(
            [target_ref[pl.ds(first + k, INNER, stride=OUTER), :] for k in (0, 1)], axis=1
        )
        residual = scale * (real * real + imag * imag - target)
        high, low = split(jnp.concatenate([residual * real, residual * imag], axis=0))
        back = dot(bh_ref[...], high) + dot(bh_ref[...], low) + dot(bl_ref[...], high)
        for k in (0, 1):
            back_ref[first + k] = back[:, tile(k)].reshape(2, INNER, INNER)
        return carry

    lax.fori_loop(0, OUTER // 2, multiply, 0)

    def backward(step, carry):
        rows = row_block(step)

        def load(k):
            cos, sin = tw_ref[0, k, rows, :], tw_ref[1, k, rows, :]
            real, imag = back_ref[k, 0, rows, :], back_ref[k, 1, rows, :]
            return real * cos + imag * sin, imag * cos - real * sin

        def store(k, value):
            for side in (0, 1):
                out_ref[step * 4 + k % 4, side, tile_rows(k // 4), :] = value[side]

        dft32(load, store, mid_ref, 1)
        return carry

    lax.fori_loop(0, INNER // BLOCK, backward, 0)


def tile_rows(index):
    return slice(index * BLOCK, (index + 1) * BLOCK)


def gradient_kernel(in_ref, wave_ref, tw_ref, dft_ref, out_ref, high_ref, low_ref, mid_ref, back_ref):
    high_ref[...], low_ref[...] = split(dft_ref[...])

    def multiply(step, carry):
        group = pl.ds(step * 4, 4)
        both = jnp.concatenate([in_ref[group, 0], in_ref[group, 1]], axis=-1).reshape(4 * INNER, 2 * INNER)
        high, low = split(both)
        out = dot(high, high_ref[...]) + dot(low, high_ref[...]) + dot(high, low_ref[...])
        back_ref[group] = out.reshape(4, INNER, 2 * INNER)
        return carry

    lax.fori_loop(0, OUTER // 4, multiply, 0)

    def block(step, carry):
        rows = row_block(step)

        def load(k):
            cos, sin = tw_ref[0, k : k + 1, :], tw_ref[1, k : k + 1, :]
            real, imag = back_ref[k, rows, tile(0)], back_ref[k, rows, tile(1)]
            return real * cos + imag * sin, imag * cos - real * sin

        def store(k, value):
            out_ref[rows, tile(k)] = value[1] * wave_ref[0, rows, tile(k)] - value[0] * wave_ref[1, rows, tile(k)]

        dft32(load, store, mid_ref, 1)
        return carry

    lax.fori_loop(0, INNER // BLOCK, block, 0)


def call(kernel, out_shapes, scratch, *args):
    return pl.pallas_call(
        kernel,
        out_shape=[jax.ShapeDtypeStruct(shape, F32) for shape in out_shapes],
        in_specs=[pl.BlockSpec(memory_space=pltpu.VMEM)] * len(args),
        out_specs=[pl.BlockSpec(memory_space=pltpu.VMEM)] * len(out_shapes),
        scratch_shapes=[pltpu.VMEM(shape, dtype) for shape, dtype in scratch],
        compiler_params=pltpu.CompilerParams(vmem_limit_bytes=40 * 2**20),
    )(*args)


def inverse_odd(value, modulus):
    result = value
    for _ in range(4):
        result = result * ((2 - value * result) % modulus) % modulus
    return result


def turns_of(steps, modulus):
    return steps.astype(F32) * (1.0 / modulus)


def table(weight, length, sign):
    index = jnp.arange(INNER, dtype=jnp.int32)
    steps = (index[:, None] * index[None, :] % INNER) * (weight % INNER) % INNER
    angle = steps.astype(F32) * (sign * 2.0 * math.pi / INNER)
    cos, sin = jnp.cos(angle) / math.sqrt(length), jnp.sin(angle) / math.sqrt(length)
    return jnp.block([[cos, sin], [-sin, cos]])


def on_device(phase, depths, targets):
    rows_dev, length = phase.shape
    planes = lax.axis_size("xl") * lax.axis_size("y")
    layers = lax.axis_size("z")
    place = lax.axis_index("xl") * lax.axis_size("y") + lax.axis_index("y")
    slab_size = math.prod(lax.axis_size(axis) for axis in SLAB)
    modulus = 2 * length

    share = rows_dev // planes
    mine = lax.dynamic_slice_in_dim(phase, place * share, share, 0)
    rows_phase = lax.all_gather(mine, "z", axis=0, tiled=True)

    all_depths = lax.all_gather(depths, ("xl", "y"), axis=0, tiled=True)
    depth = lax.dynamic_index_in_dim(all_depths, lax.axis_index("z"), keepdims=False)
    (sorted_targets,) = call(
        sort_kernel,
        [(slab_size, rows_dev, INNER)],
        [((length, rows_dev), F32)],
        targets[0],
    )
    sorted_targets = lax.all_to_all(sorted_targets, SLAB, 0, 0, tiled=True)
    sorted_targets = lax.all_to_all(sorted_targets, "z", 0, 0, tiled=True).reshape(length, INNER)

    strength = ((depth + 8) * (length // 64) + 1) % modulus
    weight = inverse_odd(strength, modulus)

    pixel = jnp.arange(length, dtype=jnp.int32)
    chirp = turns_of(pixel * pixel % modulus * weight % modulus, modulus)
    slot = lax.axis_index("xh") * lax.axis_size("c") + lax.axis_index("c")
    local = jnp.arange(layers * share, dtype=jnp.int32)
    row = (local // share * (length // layers)) + slot * rows_dev + place * share + local % share
    row_chirp = turns_of(row * row % modulus * weight % modulus, modulus)
    row_chirp = jnp.broadcast_to(row_chirp[:, None], (layers * share, INNER))

    outer = jnp.arange(OUTER, dtype=jnp.int32)[:, None]
    inner = jnp.arange(INNER, dtype=jnp.int32)[None, :]
    angle = (outer * inner * weight % length).astype(F32) * (-2.0 * math.pi / length)
    twiddle = jnp.stack([jnp.cos(angle), jnp.sin(angle)])
    tall_twiddle = jnp.broadcast_to(twiddle[:, :, :, None], (2, OUTER, INNER, INNER))
    there = table(weight, length, -1.0)
    back = table(weight, length, 1.0)

    mid = ((OUTER, 2, BLOCK, INNER), F32)
    matrix = ((2 * INNER, 2 * INNER), BF16)
    chunks = (slab_size, 2, layers * share, INNER)
    spectrum, wave = call(
        rows_kernel,
        [chunks, (2, layers * share, length)],
        [matrix, matrix, mid, ((OUTER, INNER, 2 * INNER), BF16), ((OUTER, INNER, 2 * INNER), BF16)],
        rows_phase,
        row_chirp,
        chirp[None, :],
        twiddle,
        there,
    )
    spectrum = lax.all_to_all(spectrum, SLAB, 0, 0, tiled=True)
    (spectrum,) = call(
        lambda *refs: columns_kernel(4.0 / planes, *refs),
        [chunks],
        [
            matrix,
            matrix,
            matrix,
            matrix,
            mid,
            ((OUTER, 2, INNER, INNER), BF16),
            ((OUTER, 2, INNER, INNER), BF16),
            ((OUTER, 2, INNER, INNER), F32),
        ],
        spectrum,
        sorted_targets,
        tall_twiddle,
        there,
        back,
    )
    spectrum = lax.all_to_all(spectrum, SLAB, 0, 0, tiled=True)
    (part,) = call(
        gradient_kernel,
        [(layers * share, length)],
        [matrix, matrix, mid, ((OUTER, INNER, 2 * INNER), F32)],
        spectrum,
        wave,
        twiddle,
        back,
    )
    part = lax.psum_scatter(part, "z", scatter_dimension=0, tiled=True)
    part = jnp.broadcast_to(part[None], (planes, share, length))
    return lax.all_to_all(part, ("xl", "y"), 0, 0, tiled=True).reshape(rows_dev, length)


def solution(mesh):
    fine = Mesh(mesh.devices.reshape(2, 4, 8, 2, 2), ("xl", "y", "z", "xh", "c"))
    rows = ("z", "xh", "c")
    placed = (P(rows, None), P(("xl", "y")), P(("xl", "y"), rows, None))
    return jax.shard_map(on_device, mesh=fine, in_specs=placed, out_specs=P(rows, None), check_vma=False)
```

```python
import math

import jax
import jax.numpy as jnp
import numpy as np
from jax import lax
from jax.experimental import pallas as pl
from jax.experimental.pallas import tpu as pltpu
from jax.sharding import Mesh
from jax.sharding import PartitionSpec as P

SLAB = ("xl", "y", "xh", "c")
OUTER = 32
INNER = 128
BLOCK = 16
WIDE = 4
F32 = jnp.float32
BF16 = jnp.bfloat16


def fit(function, count, odd):
    points = np.cos(np.pi * (np.arange(400) + 0.5) / 400) * 0.5
    powers = np.stack([points ** (2 * k + odd) for k in range(count)], axis=1)
    return [float(c) for c in np.linalg.lstsq(powers, function(np.pi * points), rcond=None)[0]]


SIN_TERMS = fit(np.sin, 6, 1)
COS_TERMS = fit(np.cos, 6, 0)


def horner(terms, square):
    total = jnp.full_like(square, terms[-1])
    for term in terms[-2::-1]:
        total = total * square + term
    return total


def unit_wave(turns):
    turns = turns - jnp.round(turns)
    square = turns * turns
    half_sin = turns * horner(SIN_TERMS, square)
    half_cos = horner(COS_TERMS, square)
    twice = half_sin + half_sin
    return 1.0 - twice * half_sin, twice * half_cos


def spin(value, step, size, sign):
    real, imag = value
    step = step % size
    if step == 0:
        return value
    if 4 * step == size:
        return (-imag, real) if sign > 0 else (imag, -real)
    if 2 * step == size:
        return (-real, -imag)
    if 4 * step == 3 * size:
        return (imag, -real) if sign > 0 else (-imag, real)
    cos = math.cos(2 * math.pi * step / size)
    sin = sign * math.sin(2 * math.pi * step / size)
    if 8 * step % size == 0 and abs(abs(cos) - abs(sin)) < 1e-9:
        root = abs(cos)
        real, imag = real * root, imag * root
        cs = 1 if cos > 0 else -1
        ss = 1 if sin > 0 else -1
        a = real if cs > 0 else -real
        new_real = a - imag if ss > 0 else a + imag
        b = imag if cs > 0 else -imag
        new_imag = b + real if ss > 0 else b - real
        return new_real, new_imag
    return real * cos - imag * sin, real * sin + imag * cos


def small_dft(values, sign):
    size = len(values)
    if size == 1:
        return values
    even = small_dft(values[0::2], sign)
    odd = small_dft(values[1::2], sign)
    low, high = [], []
    for k in range(size // 2):
        turned = spin(odd[k], k, size, sign)
        low.append((even[k][0] + turned[0], even[k][1] + turned[1]))
        high.append((even[k][0] - turned[0], even[k][1] - turned[1]))
    return low + high


def dft32(load, store, mid_ref, sign):
    for b in range(8):
        out = small_dft([load(8 * a + b) for a in range(4)], sign)
        for p in range(4):
            real, imag = spin(out[p], b * p, 32, sign)
            mid_ref[8 * p + b, 0] = real
            mid_ref[8 * p + b, 1] = imag
    for p in range(4):
        out = small_dft([(mid_ref[8 * p + b, 0], mid_ref[8 * p + b, 1]) for b in range(8)], sign)
        for s in range(8):
            store(p + 4 * s, out[s])


def split(value):
    high = value.astype(BF16)
    return high, (value - high.astype(F32)).astype(BF16)


def dot(left, right):
    return jnp.dot(left, right, preferred_element_type=F32)


def row_block(step):
    return pl.ds(pl.multiple_of(step * BLOCK, BLOCK), BLOCK)


def tile(index):
    return slice(index * INNER, (index + 1) * INNER)


def sort_kernel(target_ref, out_ref, turned_ref):
    for k in range(OUTER):
        turned_ref[tile(k), :] = target_ref[:, tile(k)].T
    for j in range(OUTER):
        out_ref[j] = turned_ref[pl.ds(j, INNER, stride=OUTER), :].T


def rows_kernel(phase_ref, row_ref, col_ref, tw_ref, dft_ref, out_hbm, wave_hbm, high_ref, low_ref, mid_ref, sh_ref, sl_ref, out_ref, wave_ref, sem):
    high_ref[...], low_ref[...] = split(dft_ref[...])

    def save_wave(step):
        rows = row_block(step)
        return pltpu.make_async_copy(wave_ref.at[:, rows, :], wave_hbm.at[:, rows, :], sem.at[0])

    def save_out(step):
        group = pl.ds(step * 4, 4)
        return pltpu.make_async_copy(out_ref.at[group], out_hbm.at[group], sem.at[1])

    def block(step, carry):
        rows = row_block(step)
        row_turn = row_ref[rows, :]

        def load(k):
            turns = phase_ref[rows, tile(k)] * (0.5 / math.pi) + (row_turn + col_ref[:, tile(k)])
            cos, sin = unit_wave(turns)
            wave_ref[0, rows, tile(k)] = cos
            wave_ref[1, rows, tile(k)] = sin
            return cos, sin

        def store(k, value):
            cos, sin = tw_ref[0, k : k + 1, :], tw_ref[1, k : k + 1, :]
            real, imag = value
            for part, side in ((real * cos - imag * sin, 0), (real * sin + imag * cos, 1)):
                high, low = split(part)
                sh_ref[k, rows, tile(side)] = high
                sl_ref[k, rows, tile(side)] = low

        dft32(load, store, mid_ref, -1)
        save_wave(step).start()
        return carry

    lax.fori_loop(0, INNER // BLOCK, block, 0)

    def multiply(step, carry):
        group = pl.ds(step * 4, 4)
        high = sh_ref[group].reshape(4 * INNER, 2 * INNER)
        low = sl_ref[group].reshape(4 * INNER, 2 * INNER)
        out = dot(high, high_ref[...]) + dot(low, high_ref[...]) + dot(high, low_ref[...])
        out = out.reshape(4, INNER, 2 * INNER)
        out_ref[group, 0] = out[:, :, :INNER]
        out_ref[group, 1] = out[:, :, INNER:]
        save_out(step).start()
        return carry

    lax.fori_loop(0, OUTER // 4, multiply, 0)
    pltpu.make_async_copy(wave_ref, wave_hbm, sem.at[0]).wait()
    pltpu.make_async_copy(out_ref, out_hbm, sem.at[1]).wait()


def columns_kernel(
    scale, layer_ref, in_ref, *refs
):
    pieces, refs = refs[: len(refs) - 11], refs[len(refs) - 11 :]
    tw_ref, there_ref, home_ref, out_ref, there_both, home_both, mid_ref, sh_ref, sl_ref, back_ref, target_ref = refs
    for both, ref in ((there_both, home_ref), (home_both, there_ref)):
        both[: 2 * INNER, :], both[2 * INNER :, :] = split(ref[...])

    layers = len(pieces)
    run = INNER // layers
    for k, piece in enumerate(pieces):
        start = lax.rem(layer_ref[0] + (layers - k), layers) * run
        spot = pl.ds(pl.multiple_of(start, run), run)
        for u0 in range(OUTER):
            target_ref[u0, spot, :] = piece[pl.ds(u0, run, stride=OUTER), :]

    def forward(step, carry):
        rows = row_block(step)

        def load(k):
            return tuple(in_ref[step * 4 + k % 4, side, tile_rows(k // 4), :] for side in (0, 1))

        def store(k, value):
            cos, sin = tw_ref[0, rows, k : k + 1], tw_ref[1, rows, k : k + 1]
            real, imag = value
            for part, side in ((real * cos - imag * sin, 0), (real * sin + imag * cos, 1)):
                high, low = split(part)
                sh_ref[k, side, rows, :] = high
                sl_ref[k, side, rows, :] = low

        dft32(load, store, mid_ref, -1)
        return carry

    lax.fori_loop(0, INNER // BLOCK, forward, 0)

    def wide(ref, first):
        return jnp.concatenate([ref[first + k].reshape(2 * INNER, INNER) for k in range(WIDE)], axis=1)

    def product(table_ref, high, low):
        out = dot(table_ref[...], high)
        return out[: 2 * INNER] + (out[2 * INNER :] + dot(table_ref[: 2 * INNER, :], low))

    def multiply(step, carry):
        first = step * WIDE
        field = product(there_both, wide(sh_ref, first), wide(sl_ref, first))
        real, imag = field[:INNER], field[INNER:]
        target = jnp.concatenate([target_ref[first + k] for k in range(WIDE)], axis=1)
        residual = scale * (real * real + imag * imag - target)
        back = product(home_both, *split(jnp.concatenate([residual * real, residual * imag], axis=0)))
        for k in range(WIDE):
            back_ref[first + k] = back[:, tile(k)].reshape(2, INNER, INNER)
        return carry

    lax.fori_loop(0, OUTER // WIDE, multiply, 0)

    def backward(step, carry):
        rows = row_block(step)

        def load(k):
            cos, sin = tw_ref[0, rows, k : k + 1], tw_ref[1, rows, k : k + 1]
            real, imag = back_ref[k, 0, rows, :], back_ref[k, 1, rows, :]
            return real * cos + imag * sin, imag * cos - real * sin

        def store(k, value):
            for side in (0, 1):
                out_ref[step * 4 + k % 4, side, tile_rows(k // 4), :] = value[side]

        dft32(load, store, mid_ref, 1)
        return carry

    lax.fori_loop(0, INNER // BLOCK, backward, 0)


def tile_rows(index):
    return slice(index * BLOCK, (index + 1) * BLOCK)


def gradient_kernel(in_ref, wave_ref, tw_ref, dft_ref, out_ref, high_ref, low_ref, mid_ref, back_ref):
    high_ref[...], low_ref[...] = split(dft_ref[...])

    def multiply(step, carry):
        group = pl.ds(step * 4, 4)
        both = jnp.concatenate([in_ref[group, 0], in_ref[group, 1]], axis=-1).reshape(4 * INNER, 2 * INNER)
        high, low = split(both)
        out = dot(high, high_ref[...]) + dot(low, high_ref[...]) + dot(high, low_ref[...])
        back_ref[group] = out.reshape(4, INNER, 2 * INNER)
        return carry

    lax.fori_loop(0, OUTER // 4, multiply, 0)

    def block(step, carry):
        rows = row_block(step)

        def load(k):
            cos, sin = tw_ref[0, k : k + 1, :], tw_ref[1, k : k + 1, :]
            real, imag = back_ref[k, rows, tile(0)], back_ref[k, rows, tile(1)]
            return real * cos + imag * sin, imag * cos - real * sin

        def store(k, value):
            out_ref[rows, tile(k)] = value[1] * wave_ref[0, rows, tile(k)] - value[0] * wave_ref[1, rows, tile(k)]

        dft32(load, store, mid_ref, 1)
        return carry

    lax.fori_loop(0, INNER // BLOCK, block, 0)


def call(kernel, out_shapes, scratch, *args, space=pltpu.VMEM, limit=28):
    return pl.pallas_call(
        kernel,
        out_shape=[jax.ShapeDtypeStruct(shape, F32) for shape in out_shapes],
        in_specs=[pl.BlockSpec(memory_space=pltpu.SMEM if arg.dtype == jnp.int32 else pltpu.VMEM) for arg in args],
        out_specs=[pl.BlockSpec(memory_space=space)] * len(out_shapes),
        scratch_shapes=[pltpu.VMEM(*item) if isinstance(item, tuple) else item for item in scratch],
        compiler_params=pltpu.CompilerParams(vmem_limit_bytes=limit * 2**20),
    )(*args)


def inverse_odd(value, modulus):
    result = value
    for _ in range(4):
        result = result * ((2 - value * result) % modulus) % modulus
    return result


def turns_of(steps, modulus):
    return steps.astype(F32) * (1.0 / modulus)


def table(weight, length, sign):
    index = jnp.arange(INNER, dtype=jnp.int32)
    steps = (index[:, None] * index[None, :] % INNER) * (weight % INNER) % INNER
    angle = steps.astype(F32) * (sign * 2.0 * math.pi / INNER)
    cos, sin = jnp.cos(angle) / math.sqrt(length), jnp.sin(angle) / math.sqrt(length)
    return jnp.block([[cos, sin], [-sin, cos]])


def on_device(phase, depths, targets):
    rows_dev, length = phase.shape
    planes = lax.axis_size("xl") * lax.axis_size("y")
    layers = lax.axis_size("z")
    place = lax.axis_index("xl") * lax.axis_size("y") + lax.axis_index("y")
    slab_size = math.prod(lax.axis_size(axis) for axis in SLAB)
    modulus = 2 * length

    share = rows_dev // planes
    mine = lax.dynamic_slice_in_dim(phase, place * share, share, 0)
    mine, targets = lax.optimization_barrier((mine, targets))
    rows_phase = lax.all_gather(mine, "z", axis=0, tiled=True)

    all_depths = lax.all_gather(depths, ("xl", "y"), axis=0, tiled=True)
    depth = lax.dynamic_index_in_dim(all_depths, lax.axis_index("z"), keepdims=False)
    (sorted_targets,) = call(
        sort_kernel,
        [(slab_size, rows_dev, INNER)],
        [((length, rows_dev), F32)],
        targets[0],
    )
    sorted_targets = lax.all_to_all(sorted_targets, SLAB, 0, 0, tiled=True)
    rows_phase, sorted_targets = lax.optimization_barrier((rows_phase, sorted_targets))
    layer = lax.axis_index("z")
    group = slab_size // layers
    pieces = []
    for k in range(layers):
        piece = lax.dynamic_slice_in_dim(sorted_targets, (layer + k) % layers * group, group, 0)
        if k:
            piece = lax.ppermute(piece, "z", [(i, (i + k) % layers) for i in range(layers)])
        pieces.append(piece.reshape(group * rows_dev, INNER))

    strength = ((depth + 8) * (length // 64) + 1) % modulus
    weight = inverse_odd(strength, modulus)

    pixel = jnp.arange(length, dtype=jnp.int32)
    chirp = turns_of(pixel * pixel % modulus * weight % modulus, modulus)
    slot = lax.axis_index("xh") * lax.axis_size("c") + lax.axis_index("c")
    local = jnp.arange(layers * share, dtype=jnp.int32)
    row = (local // share * (length // layers)) + slot * rows_dev + place * share + local % share
    row_chirp = turns_of(row * row % modulus * weight % modulus, modulus)
    row_chirp = jnp.broadcast_to(row_chirp[:, None], (layers * share, INNER))

    outer = jnp.arange(OUTER, dtype=jnp.int32)[:, None]
    inner = jnp.arange(INNER, dtype=jnp.int32)[None, :]
    angle = (outer * inner * weight % length).astype(F32) * (-2.0 * math.pi / length)
    twiddle = jnp.stack([jnp.cos(angle), jnp.sin(angle)])
    tall_twiddle = jnp.stack([jnp.cos(angle.T), jnp.sin(angle.T)])
    there = table(weight, length, -1.0)
    back = table(weight, length, 1.0)

    mid = ((OUTER, 2, BLOCK, INNER), F32)
    matrix = ((2 * INNER, 2 * INNER), BF16)
    chunks = (slab_size, 2, layers * share, INNER)
    spectrum, wave = call(
        rows_kernel,
        [chunks, (2, layers * share, length)],
        [
            matrix,
            matrix,
            mid,
            ((OUTER, INNER, 2 * INNER), BF16),
            ((OUTER, INNER, 2 * INNER), BF16),
            (chunks, F32),
            ((2, layers * share, length), F32),
            pltpu.SemaphoreType.DMA((2,)),
        ],
        rows_phase,
        row_chirp,
        chirp[None, :],
        twiddle,
        there,
        space=pltpu.HBM,
        limit=60,
    )
    spectrum = lax.all_to_all(spectrum, SLAB, 0, 0, tiled=True)
    (spectrum,) = call(
        lambda *refs: columns_kernel(4.0 / planes, *refs),
        [chunks],
        [
            ((4 * INNER, 2 * INNER), BF16),
            ((4 * INNER, 2 * INNER), BF16),
            mid,
            ((OUTER, 2, INNER, INNER), BF16),
            ((OUTER, 2, INNER, INNER), BF16),
            ((OUTER, 2, INNER, INNER), F32),
            ((OUTER, INNER, INNER), F32),
        ],
        layer.astype(jnp.int32)[None],
        spectrum,
        *pieces,
        tall_twiddle,
        there,
        back,
    )
    spectrum = lax.all_to_all(spectrum, SLAB, 0, 0, tiled=True)
    (part,) = call(
        gradient_kernel,
        [(layers * share, length)],
        [matrix, matrix, mid, ((OUTER, INNER, 2 * INNER), F32)],
        spectrum,
        wave,
        twiddle,
        back,
    )
    part = lax.psum_scatter(part, "z", scatter_dimension=0, tiled=True)
    part = jnp.broadcast_to(part[None], (planes, share, length))
    return lax.all_to_all(part, ("xl", "y"), 0, 0, tiled=True).reshape(rows_dev, length)


def solution(mesh):
    fine = Mesh(mesh.devices.reshape(2, 4, 8, 2, 2), ("xl", "y", "z", "xh", "c"))
    rows = ("z", "xh", "c")
    placed = (P(rows, None), P(("xl", "y")), P(("xl", "y"), rows, None))
    return jax.shard_map(on_device, mesh=fine, in_specs=placed, out_specs=P(rows, None), check_vma=False)
```

```python
import functools
import math

import jax
import jax.numpy as jnp
import numpy as np
from jax import lax
from jax.experimental import pallas as pl
from jax.experimental.pallas import tpu as pltpu
from jax.sharding import Mesh
from jax.sharding import PartitionSpec as P

SLAB = ("xl", "y", "xh", "c")
OUTER = 32
INNER = 128
BLOCK = 16
WIDE = 16
NOTE = 8
F32 = jnp.float32
BF16 = jnp.bfloat16


def fit(function, count, odd):
    points = np.cos(np.pi * (np.arange(400) + 0.5) / 400) * 0.5
    powers = np.stack([points ** (2 * k + odd) for k in range(count)], axis=1)
    return [float(c) for c in np.linalg.lstsq(powers, function(np.pi * points), rcond=None)[0]]


SIN_TERMS = fit(np.sin, 6, 1)
COS_TERMS = fit(np.cos, 6, 0)


def horner(terms, square):
    total = jnp.full_like(square, terms[-1])
    for term in terms[-2::-1]:
        total = total * square + term
    return total


def unit_wave(turns):
    turns = turns - jnp.round(turns)
    square = turns * turns
    half_sin = turns * horner(SIN_TERMS, square)
    half_cos = horner(COS_TERMS, square)
    twice = half_sin + half_sin
    return 1.0 - twice * half_sin, twice * half_cos


def spin(value, step, size, sign):
    real, imag = value
    step = step % size
    if step == 0:
        return value
    if 4 * step == size:
        return (-imag, real) if sign > 0 else (imag, -real)
    if 2 * step == size:
        return (-real, -imag)
    if 4 * step == 3 * size:
        return (imag, -real) if sign > 0 else (-imag, real)
    cos = math.cos(2 * math.pi * step / size)
    sin = sign * math.sin(2 * math.pi * step / size)
    if 8 * step % size == 0 and abs(abs(cos) - abs(sin)) < 1e-9:
        root = abs(cos)
        real, imag = real * root, imag * root
        cs = 1 if cos > 0 else -1
        ss = 1 if sin > 0 else -1
        a = real if cs > 0 else -real
        new_real = a - imag if ss > 0 else a + imag
        b = imag if cs > 0 else -imag
        new_imag = b + real if ss > 0 else b - real
        return new_real, new_imag
    return real * cos - imag * sin, real * sin + imag * cos


def small_dft(values, sign):
    size = len(values)
    if size == 1:
        return values
    even = small_dft(values[0::2], sign)
    odd = small_dft(values[1::2], sign)
    low, high = [], []
    for k in range(size // 2):
        turned = spin(odd[k], k, size, sign)
        low.append((even[k][0] + turned[0], even[k][1] + turned[1]))
        high.append((even[k][0] - turned[0], even[k][1] - turned[1]))
    return low + high


def dft32(load, store, mid_ref, sign):
    for b in range(8):
        out = small_dft([load(8 * a + b) for a in range(4)], sign)
        for p in range(4):
            real, imag = spin(out[p], b * p, 32, sign)
            mid_ref[8 * p + b, 0] = real
            mid_ref[8 * p + b, 1] = imag
    for p in range(4):
        out = small_dft([(mid_ref[8 * p + b, 0], mid_ref[8 * p + b, 1]) for b in range(8)], sign)
        for s in range(8):
            store(p + 4 * s, out[s])


def split(value):
    high = value.astype(BF16)
    return high, (value - high.astype(F32)).astype(BF16)


def dot(left, right):
    return jnp.dot(left, right, preferred_element_type=F32)


def row_block(step):
    return pl.ds(pl.multiple_of(step * BLOCK, BLOCK), BLOCK)


def tile(index):
    return slice(index * INNER, (index + 1) * INNER)


def sort_kernel(depth_ref, target_ref, out_ref, turned_ref):
    for k in range(OUTER):
        turned_ref[tile(k), :] = target_ref[:, tile(k)].T
    for j in range(OUTER):
        out_ref[j, :INNER] = turned_ref[pl.ds(j, INNER, stride=OUTER), :].T
        out_ref[j, INNER:] = jnp.full((NOTE, INNER), depth_ref[0].astype(F32))


def rows_kernel(
    length, place_ref, phase_ref, targets_hbm, out_hbm, wave_hbm, tw_ref, tall_ref, dft_ref, *refs
):
    sent = refs[:-12]
    high_ref, low_ref, mid_ref, sh_ref, sl_ref, out_ref, wave_ref, row_ref, col_ref, note_ref, sem, send_sem = refs[-12:]
    layers = len(sent) + 1
    group = targets_hbm.shape[0] // layers
    layer = place_ref[0]

    note = pltpu.make_async_copy(targets_hbm.at[layer * group, pl.ds(INNER, NOTE)], note_ref, sem.at[2])
    note.start()
    sends = [
        pltpu.make_async_copy(
            targets_hbm.at[pl.ds(lax.rem(layer + k, layers) * group, group), pl.ds(0, INNER)],
            sent[k - 1],
            send_sem.at[k - 1],
        )
        for k in range(1, layers)
    ]
    for send in sends:
        send.start()
    note.wait()
    modulus = 2 * length
    weight = inverse_odd(
        ((note_ref[0:1, :].astype(jnp.int32) + 8) * (length // 64) + 1) & (modulus - 1), modulus
    )

    def index(shape, axis):
        return lax.broadcasted_iota(jnp.int32, shape, axis)

    def waves(steps, size):
        return unit_wave(steps.astype(F32) * (-1.0 / size))

    flat = (OUTER, INNER)
    tw_ref[0], tw_ref[1] = waves((index(flat, 0) * index(flat, 1) * weight) & (length - 1), length)
    tall = (INNER, OUTER)
    tall_ref[0], tall_ref[1] = waves(
        (index(tall, 0) * index(tall, 1) * weight[:, :OUTER]) & (length - 1), length
    )
    square = (INNER, INNER)
    steps = (index(square, 0) * index(square, 1)) & (INNER - 1)
    cos, sin = waves((steps * (weight & (INNER - 1))) & (INNER - 1), INNER)
    cos, sin = cos * (1.0 / math.sqrt(length)), sin * (1.0 / math.sqrt(length))
    dft_ref[:INNER, :INNER], dft_ref[:INNER, INNER:] = cos, sin
    dft_ref[INNER:, :INNER], dft_ref[INNER:, INNER:] = -sin, cos
    high_ref[...], low_ref[...] = split(dft_ref[...])

    def chirp(pixel):
        return ((((pixel * pixel) & (modulus - 1)) * weight) & (modulus - 1)).astype(F32) * (1.0 / modulus)

    col_ref[...] = chirp(index(flat, 0) * INNER + index(flat, 1))
    local = index(square, 0)
    inside = local & (BLOCK - 1)
    row_ref[...] = chirp((local - inside) * (length // layers // BLOCK) + place_ref[1] + inside)

    def save_wave(step):
        rows = row_block(step)
        return pltpu.make_async_copy(wave_ref.at[:, rows, :], wave_hbm.at[:, rows, :], sem.at[0])

    def save_out(step):
        group = pl.ds(step * 4, 4)
        return pltpu.make_async_copy(out_ref.at[group], out_hbm.at[group], sem.at[1])

    def block(step, carry):
        rows = row_block(step)
        row_turn = row_ref[rows, :]

        def load(k):
            turns = phase_ref[rows, tile(k)] * (0.5 / math.pi) + (row_turn + col_ref[k : k + 1, :])
            cos, sin = unit_wave(turns)
            wave_ref[0, rows, tile(k)] = cos
            wave_ref[1, rows, tile(k)] = sin
            return cos, sin

        def store(k, value):
            cos, sin = tw_ref[0, k : k + 1, :], tw_ref[1, k : k + 1, :]
            real, imag = value
            for part, side in ((real * cos - imag * sin, 0), (real * sin + imag * cos, 1)):
                high, low = split(part)
                sh_ref[k, rows, tile(side)] = high
                sl_ref[k, rows, tile(side)] = low

        dft32(load, store, mid_ref, -1)
        save_wave(step).start()
        return carry

    lax.fori_loop(0, INNER // BLOCK, block, 0)

    def multiply(step, carry):
        group = pl.ds(step * 4, 4)
        high = sh_ref[group].reshape(4 * INNER, 2 * INNER)
        low = sl_ref[group].reshape(4 * INNER, 2 * INNER)
        out = dot(
            jnp.concatenate([high, low, high], axis=1),
            jnp.concatenate([high_ref[...], high_ref[...], low_ref[...]], axis=0),
        )
        out = out.reshape(4, INNER, 2 * INNER)
        out_ref[group, 0] = out[:, :, :INNER]
        out_ref[group, 1] = out[:, :, INNER:]
        save_out(step).start()
        return carry

    lax.fori_loop(0, OUTER // 4, multiply, 0)
    pltpu.make_async_copy(wave_ref, wave_hbm, sem.at[0]).wait()
    pltpu.make_async_copy(out_ref, out_hbm, sem.at[1]).wait()
    for send in sends:
        send.wait()


def columns_kernel(
    scale, layer_ref, tw_ref, there_ref, in_hbm, *refs
):
    pieces_hbm, refs = refs[: len(refs) - 11], refs[len(refs) - 11 :]
    out_ref, there_both, home_both, mid_ref, sh_ref, sl_ref, back_ref, target_ref, in_ref, pieces_ref, sem = refs
    layers = len(pieces_hbm)
    run = INNER // layers

    def fetch(step):
        group = pl.ds(step * 4, 4)
        return pltpu.make_async_copy(in_hbm.at[group], in_ref.at[group], sem.at[step])

    def fetch_piece(k):
        return pltpu.make_async_copy(pieces_hbm[k], pieces_ref.at[k], sem.at[INNER // BLOCK + k])

    for step in range(INNER // BLOCK):
        fetch(step).start()
    for k in range(layers):
        fetch_piece(k).start()

    for both, matrix in ((there_both, transposed(there_ref)), (home_both, there_ref[...])):
        high, low = split(matrix)
        both[...] = jnp.concatenate([high, low, high], axis=1)

    def forward(step, carry):
        rows = row_block(step)
        fetch(step).wait()

        def load(k):
            return tuple(in_ref[step * 4 + k % 4, side, tile_rows(k // 4), :] for side in (0, 1))

        def store(k, value):
            cos, sin = tw_ref[0, rows, k : k + 1], tw_ref[1, rows, k : k + 1]
            real, imag = value
            for part, side in ((real * cos - imag * sin, 0), (real * sin + imag * cos, 1)):
                high, low = split(part)
                sh_ref[k, side, rows, :] = high
                sl_ref[k, side, rows, :] = low

        dft32(load, store, mid_ref, -1)
        return carry

    lax.fori_loop(0, INNER // BLOCK, forward, 0)

    for k in range(layers):
        fetch_piece(k).wait()
        start = lax.rem(layer_ref[0] + (layers - k), layers) * run
        spot = pl.ds(pl.multiple_of(start, run), run)
        for u0 in range(OUTER):
            target_ref[u0, spot, :] = pieces_ref[k, pl.ds(u0, run, stride=OUTER), :]

    def wide(ref, first):
        return jnp.concatenate([ref[first + k].reshape(2 * INNER, INNER) for k in range(WIDE)], axis=1)

    def product(table_ref, high, low):
        return dot(table_ref[...], jnp.concatenate([high, high, low], axis=0))

    def multiply(step, carry):
        first = step * WIDE
        field = product(there_both, wide(sh_ref, first), wide(sl_ref, first))
        real, imag = field[:INNER], field[INNER:]
        target = jnp.concatenate([target_ref[first + k] for k in range(WIDE)], axis=1)
        residual = scale * (real * real + imag * imag - target)
        back = product(home_both, *split(jnp.concatenate([residual * real, residual * imag], axis=0)))
        for k in range(WIDE):
            back_ref[first + k] = back[:, tile(k)].reshape(2, INNER, INNER)
        return carry

    lax.fori_loop(0, OUTER // WIDE, multiply, 0)

    def backward(step, carry):
        rows = row_block(step)

        def load(k):
            cos, sin = tw_ref[0, rows, k : k + 1], tw_ref[1, rows, k : k + 1]
            real, imag = back_ref[k, 0, rows, :], back_ref[k, 1, rows, :]
            return real * cos + imag * sin, imag * cos - real * sin

        def store(k, value):
            for side in (0, 1):
                out_ref[step * 4 + k % 4, side, tile_rows(k // 4), :] = value[side]

        dft32(load, store, mid_ref, 1)
        return carry

    lax.fori_loop(0, INNER // BLOCK, backward, 0)


def transposed(ref):
    return jnp.concatenate(
        [
            jnp.concatenate([ref[:INNER, :INNER], ref[INNER:, :INNER]], axis=1),
            jnp.concatenate([ref[:INNER, INNER:], ref[INNER:, INNER:]], axis=1),
        ],
        axis=0,
    )


def tile_rows(index):
    return slice(index * BLOCK, (index + 1) * BLOCK)


def gradient_kernel(in_ref, wave_ref, tw_ref, dft_ref, out_ref, high_ref, low_ref, mid_ref, back_ref):
    high_ref[...], low_ref[...] = split(transposed(dft_ref))

    def multiply(step, carry):
        group = pl.ds(step * 4, 4)
        both = jnp.concatenate([in_ref[group, 0], in_ref[group, 1]], axis=-1).reshape(4 * INNER, 2 * INNER)
        high, low = split(both)
        out = dot(
            jnp.concatenate([high, low, high], axis=1),
            jnp.concatenate([high_ref[...], high_ref[...], low_ref[...]], axis=0),
        )
        back_ref[group] = out.reshape(4, INNER, 2 * INNER)
        return carry

    lax.fori_loop(0, OUTER // 4, multiply, 0)

    def block(step, carry):
        rows = row_block(step)

        def load(k):
            cos, sin = tw_ref[0, k : k + 1, :], tw_ref[1, k : k + 1, :]
            real, imag = back_ref[k, rows, tile(0)], back_ref[k, rows, tile(1)]
            return real * cos + imag * sin, imag * cos - real * sin

        def store(k, value):
            out_ref[rows, tile(k)] = value[1] * wave_ref[0, rows, tile(k)] - value[0] * wave_ref[1, rows, tile(k)]

        dft32(load, store, mid_ref, 1)
        return carry

    lax.fori_loop(0, INNER // BLOCK, block, 0)


def call(kernel, out_shapes, scratch, *args, direct=(), limit=28, held=0):
    return pl.pallas_call(
        kernel,
        out_shape=[jax.ShapeDtypeStruct(shape, F32) for shape in out_shapes],
        in_specs=[
            pl.BlockSpec(
                memory_space=pltpu.SMEM if arg.dtype == jnp.int32 else pl.ANY if k >= len(args) - held else pltpu.VMEM
            )
            for k, arg in enumerate(args)
        ],
        out_specs=[pl.BlockSpec(memory_space=pltpu.HBM if k in direct else pltpu.VMEM) for k in range(len(out_shapes))],
        scratch_shapes=[pltpu.VMEM(*item) if isinstance(item, tuple) else item for item in scratch],
        compiler_params=pltpu.CompilerParams(vmem_limit_bytes=limit * 2**20),
    )(*args)


def inverse_odd(value, modulus):
    result = value
    for _ in range(4):
        result = (result * ((2 - value * result) & (modulus - 1))) & (modulus - 1)
    return result


def on_device(phase, depths, targets):
    rows_dev, length = phase.shape
    planes = lax.axis_size("xl") * lax.axis_size("y")
    layers = lax.axis_size("z")
    place = lax.axis_index("xl") * lax.axis_size("y") + lax.axis_index("y")
    slab_size = math.prod(lax.axis_size(axis) for axis in SLAB)
    share = rows_dev // planes
    mine = lax.dynamic_slice_in_dim(phase, place * share, share, 0)
    mine, targets = lax.optimization_barrier((mine, targets))
    rows_phase = lax.all_gather(mine, "z", axis=0, tiled=True)

    (sorted_targets,) = call(
        sort_kernel,
        [(slab_size, rows_dev + NOTE, INNER)],
        [((length, rows_dev), F32)],
        depths,
        targets[0],
        limit=60,
    )
    sorted_targets = lax.all_to_all(sorted_targets, SLAB, 0, 0, tiled=True)
    layer = lax.axis_index("z")
    group = slab_size // layers
    layer_index = layer.astype(jnp.int32)
    first_row = (lax.axis_index("xh") * lax.axis_size("c") + lax.axis_index("c")) * rows_dev + place * share

    mid = ((OUTER, 2, BLOCK, INNER), F32)
    matrix = ((2 * INNER, 2 * INNER), BF16)
    chunks = (slab_size, 2, layers * share, INNER)
    spectrum, wave, twiddle, tall_twiddle, there, *sent = call(
        functools.partial(rows_kernel, length),
        [
            chunks,
            (2, layers * share, length),
            (2, OUTER, INNER),
            (2, INNER, OUTER),
            (2 * INNER, 2 * INNER),
        ]
        + [(group, rows_dev, INNER)] * (layers - 1),
        [
            matrix,
            matrix,
            mid,
            ((OUTER, INNER, 2 * INNER), BF16),
            ((OUTER, INNER, 2 * INNER), BF16),
            (chunks, F32),
            ((2, layers * share, length), F32),
            ((INNER, INNER), F32),
            ((OUTER, INNER), F32),
            ((NOTE, INNER), F32),
            pltpu.SemaphoreType.DMA((3,)),
            pltpu.SemaphoreType.DMA((layers - 1,)),
        ],
        jnp.stack([layer_index, first_row.astype(jnp.int32)]),
        rows_phase,
        sorted_targets,
        held=1,
        direct=(0, 1) + tuple(range(5, 4 + layers)),
        limit=60,
    )
    own = lax.dynamic_slice(sorted_targets, (layer * group, 0, 0), (group, rows_dev, INNER))
    pieces = [own] + [
        lax.ppermute(piece, "z", [(i, (i + k) % layers) for i in range(layers)]) for k, piece in enumerate(sent, 1)
    ]
    pieces = [piece.reshape(group * rows_dev, INNER) for piece in pieces]
    spectrum = lax.all_to_all(spectrum, SLAB, 0, 0, tiled=True)
    (spectrum,) = call(
        lambda *refs: columns_kernel(4.0 / planes, *refs),
        [chunks],
        [
            ((2 * INNER, 6 * INNER), BF16),
            ((2 * INNER, 6 * INNER), BF16),
            mid,
            ((OUTER, 2, INNER, INNER), BF16),
            ((OUTER, 2, INNER, INNER), BF16),
            ((OUTER, 2, INNER, INNER), F32),
            ((OUTER, INNER, INNER), F32),
            (chunks, F32),
            ((layers, group * rows_dev, INNER), F32),
            pltpu.SemaphoreType.DMA((INNER // BLOCK + layers,)),
        ],
        layer_index[None],
        tall_twiddle,
        there,
        spectrum,
        *pieces,
        held=1 + layers,
    )
    spectrum = lax.all_to_all(spectrum, SLAB, 0, 0, tiled=True)
    (part,) = call(
        gradient_kernel,
        [(layers * share, length)],
        [matrix, matrix, mid, ((OUTER, INNER, 2 * INNER), F32)],
        spectrum,
        wave,
        twiddle,
        there,
    )
    part = lax.psum_scatter(part, "z", scatter_dimension=0, tiled=True)
    part = jnp.broadcast_to(part[None], (planes, share, length))
    return lax.all_to_all(part, ("xl", "y"), 0, 0, tiled=True).reshape(rows_dev, length)


def solution(mesh):
    fine = Mesh(mesh.devices.reshape(2, 4, 8, 2, 2), ("xl", "y", "z", "xh", "c"))
    rows = ("z", "xh", "c")
    placed = (P(rows, None), P(("xl", "y")), P(("xl", "y"), rows, None))
    return jax.shard_map(on_device, mesh=fine, in_specs=placed, out_specs=P(rows, None), check_vma=False)
```

```python
import functools
import math

import jax
import jax.numpy as jnp
import numpy as np
from jax import lax
from jax.experimental import pallas as pl
from jax.experimental.pallas import tpu as pltpu
from jax.sharding import Mesh
from jax.sharding import PartitionSpec as P

SLAB = ("xl", "y", "xh", "c")
OUTER = 32
INNER = 128
BLOCK = 16
WIDE = 16
NOTE = 8
F32 = jnp.float32
BF16 = jnp.bfloat16


def fit(function, count, odd):
    points = np.cos(np.pi * (np.arange(400) + 0.5) / 400) * 0.5
    powers = np.stack([points ** (2 * k + odd) for k in range(count)], axis=1)
    return [float(c) for c in np.linalg.lstsq(powers, function(np.pi * points), rcond=None)[0]]


SIN_TERMS = fit(np.sin, 6, 1)
COS_TERMS = fit(np.cos, 6, 0)


def horner(terms, square):
    total = jnp.full_like(square, terms[-1])
    for term in terms[-2::-1]:
        total = total * square + term
    return total


def unit_wave(turns):
    turns = turns - jnp.round(turns)
    square = turns * turns
    half_sin = turns * horner(SIN_TERMS, square)
    half_cos = horner(COS_TERMS, square)
    twice = half_sin + half_sin
    return 1.0 - twice * half_sin, twice * half_cos


def spin(value, step, size, sign):
    real, imag = value
    step = step % size
    if step == 0:
        return value
    if 4 * step == size:
        return (-imag, real) if sign > 0 else (imag, -real)
    if 2 * step == size:
        return (-real, -imag)
    if 4 * step == 3 * size:
        return (imag, -real) if sign > 0 else (-imag, real)
    cos = math.cos(2 * math.pi * step / size)
    sin = sign * math.sin(2 * math.pi * step / size)
    if 8 * step % size == 0 and abs(abs(cos) - abs(sin)) < 1e-9:
        root = abs(cos)
        real, imag = real * root, imag * root
        cs = 1 if cos > 0 else -1
        ss = 1 if sin > 0 else -1
        a = real if cs > 0 else -real
        new_real = a - imag if ss > 0 else a + imag
        b = imag if cs > 0 else -imag
        new_imag = b + real if ss > 0 else b - real
        return new_real, new_imag
    return real * cos - imag * sin, real * sin + imag * cos


def small_dft(values, sign):
    size = len(values)
    if size == 1:
        return values
    even = small_dft(values[0::2], sign)
    odd = small_dft(values[1::2], sign)
    low, high = [], []
    for k in range(size // 2):
        turned = spin(odd[k], k, size, sign)
        low.append((even[k][0] + turned[0], even[k][1] + turned[1]))
        high.append((even[k][0] - turned[0], even[k][1] - turned[1]))
    return low + high


def dft32(load, store, mid_ref, sign):
    for b in range(8):
        out = small_dft([load(8 * a + b) for a in range(4)], sign)
        for p in range(4):
            real, imag = spin(out[p], b * p, 32, sign)
            mid_ref[8 * p + b, 0] = real
            mid_ref[8 * p + b, 1] = imag
    for p in range(4):
        out = small_dft([(mid_ref[8 * p + b, 0], mid_ref[8 * p + b, 1]) for b in range(8)], sign)
        for s in range(8):
            store(p + 4 * s, out[s])


def split(value):
    high = value.astype(BF16)
    return high, (value - high.astype(F32)).astype(BF16)


def dot(left, right):
    return jnp.dot(left, right, preferred_element_type=F32)


def row_block(step):
    return pl.ds(pl.multiple_of(step * BLOCK, BLOCK), BLOCK)


def tile(index):
    return slice(index * INNER, (index + 1) * INNER)


def sort_kernel(depth_ref, target_ref, out_ref, turned_ref):
    for k in range(OUTER):
        turned_ref[tile(k), :] = target_ref[:, tile(k)].T
    for j in range(OUTER):
        out_ref[j, :INNER] = turned_ref[pl.ds(j, INNER, stride=OUTER), :].T
        out_ref[j, INNER:] = jnp.full((NOTE, INNER), depth_ref[0].astype(F32))


def rows_kernel(
    length, place_ref, phase_ref, targets_hbm, out_hbm, wave_hbm, tw_ref, tall_ref, dft_ref, *refs
):
    sent = refs[:-13]
    high_ref, low_ref, mid_ref, sh_ref, sl_ref, out_ref, wave_ref, row_ref, col_ref, note_ref, stage_ref, sem, send_sem = refs[-13:]
    layers = len(sent) + 1
    group = targets_hbm.shape[0] // layers
    layer = place_ref[0]

    note = pltpu.make_async_copy(targets_hbm.at[layer * group, pl.ds(INNER, NOTE)], note_ref, sem.at[2])
    note.start()
    stage = pltpu.make_async_copy(targets_hbm.at[:, pl.ds(0, INNER)], stage_ref, sem.at[3])
    stage.start()
    sends = [
        pltpu.make_async_copy(
            stage_ref.at[pl.ds(lax.rem(layer + k, layers) * group, group)],
            sent[k - 1],
            send_sem.at[k - 1],
        )
        for k in range(1, layers)
    ]
    note.wait()
    modulus = 2 * length
    weight = inverse_odd(
        ((note_ref[0:1, :].astype(jnp.int32) + 8) * (length // 64) + 1) & (modulus - 1), modulus
    )

    def index(shape, axis):
        return lax.broadcasted_iota(jnp.int32, shape, axis)

    def waves(steps, size):
        return unit_wave(steps.astype(F32) * (-1.0 / size))

    flat = (OUTER, INNER)
    tw_ref[0], tw_ref[1] = waves((index(flat, 0) * index(flat, 1) * weight) & (length - 1), length)
    tall = (INNER, OUTER)
    tall_ref[0], tall_ref[1] = waves(
        (index(tall, 0) * index(tall, 1) * weight[:, :OUTER]) & (length - 1), length
    )
    square = (INNER, INNER)
    steps = (index(square, 0) * index(square, 1)) & (INNER - 1)
    cos, sin = waves((steps * (weight & (INNER - 1))) & (INNER - 1), INNER)
    cos, sin = cos * (1.0 / math.sqrt(length)), sin * (1.0 / math.sqrt(length))
    dft_ref[:INNER, :INNER], dft_ref[:INNER, INNER:] = cos, sin
    dft_ref[INNER:, :INNER], dft_ref[INNER:, INNER:] = -sin, cos
    high_ref[...], low_ref[...] = split(dft_ref[...])

    def chirp(pixel):
        return ((((pixel * pixel) & (modulus - 1)) * weight) & (modulus - 1)).astype(F32) * (1.0 / modulus)

    col_ref[...] = chirp(index(flat, 0) * INNER + index(flat, 1))
    local = index(square, 0)
    inside = local & (BLOCK - 1)
    row_ref[...] = chirp((local - inside) * (length // layers // BLOCK) + place_ref[1] + inside)

    stage.wait()
    for send in sends:
        send.start()

    def save_wave(step):
        rows = row_block(step)
        return pltpu.make_async_copy(wave_ref.at[:, rows, :], wave_hbm.at[:, rows, :], sem.at[0])

    def save_out(step):
        group = pl.ds(step * 4, 4)
        return pltpu.make_async_copy(out_ref.at[group], out_hbm.at[group], sem.at[1])

    def block(step, carry):
        rows = row_block(step)
        row_turn = row_ref[rows, :]

        def load(k):
            turns = phase_ref[rows, tile(k)] * (0.5 / math.pi) + (row_turn + col_ref[k : k + 1, :])
            cos, sin = unit_wave(turns)
            wave_ref[0, rows, tile(k)] = cos
            wave_ref[1, rows, tile(k)] = sin
            return cos, sin

        def store(k, value):
            cos, sin = tw_ref[0, k : k + 1, :], tw_ref[1, k : k + 1, :]
            real, imag = value
            for part, side in ((real * cos - imag * sin, 0), (real * sin + imag * cos, 1)):
                high, low = split(part)
                sh_ref[k, rows, tile(side)] = high
                sl_ref[k, rows, tile(side)] = low

        dft32(load, store, mid_ref, -1)
        save_wave(step).start()
        return carry

    lax.fori_loop(0, INNER // BLOCK, block, 0)

    def multiply(step, carry):
        group = pl.ds(step * 4, 4)
        high = sh_ref[group].reshape(4 * INNER, 2 * INNER)
        low = sl_ref[group].reshape(4 * INNER, 2 * INNER)
        out = dot(
            jnp.concatenate([high, low, high], axis=1),
            jnp.concatenate([high_ref[...], high_ref[...], low_ref[...]], axis=0),
        )
        out = out.reshape(4, INNER, 2 * INNER)
        out_ref[group, 0] = out[:, :, :INNER]
        out_ref[group, 1] = out[:, :, INNER:]
        save_out(step).start()
        return carry

    lax.fori_loop(0, OUTER // 4, multiply, 0)
    pltpu.make_async_copy(wave_ref, wave_hbm, sem.at[0]).wait()
    pltpu.make_async_copy(out_ref, out_hbm, sem.at[1]).wait()
    for send in sends:
        send.wait()


def columns_kernel(
    scale, layer_ref, tw_ref, there_ref, in_hbm, *refs
):
    pieces_hbm, refs = refs[: len(refs) - 11], refs[len(refs) - 11 :]
    out_ref, there_both, home_both, mid_ref, sh_ref, sl_ref, back_ref, target_ref, in_ref, pieces_ref, sem = refs
    layers = len(pieces_hbm)
    run = INNER // layers

    def fetch(step):
        group = pl.ds(step * 4, 4)
        return pltpu.make_async_copy(in_hbm.at[group], in_ref.at[group], sem.at[step])

    def fetch_piece(k):
        return pltpu.make_async_copy(pieces_hbm[k], pieces_ref.at[k], sem.at[INNER // BLOCK + k])

    for step in range(INNER // BLOCK):
        fetch(step).start()
    for k in range(layers):
        fetch_piece(k).start()

    for both, matrix in ((there_both, transposed(there_ref)), (home_both, there_ref[...])):
        high, low = split(matrix)
        both[...] = jnp.concatenate([high, low, high], axis=1)

    def forward(step, carry):
        rows = row_block(step)
        fetch(step).wait()

        def load(k):
            return tuple(in_ref[step * 4 + k % 4, side, tile_rows(k // 4), :] for side in (0, 1))

        def store(k, value):
            cos, sin = tw_ref[0, rows, k : k + 1], tw_ref[1, rows, k : k + 1]
            real, imag = value
            for part, side in ((real * cos - imag * sin, 0), (real * sin + imag * cos, 1)):
                high, low = split(part)
                sh_ref[k, side, rows, :] = high
                sl_ref[k, side, rows, :] = low

        dft32(load, store, mid_ref, -1)
        return carry

    lax.fori_loop(0, INNER // BLOCK, forward, 0)

    for k in range(layers):
        fetch_piece(k).wait()
        start = lax.rem(layer_ref[0] + (layers - k), layers) * run
        spot = pl.ds(pl.multiple_of(start, run), run)
        for u0 in range(OUTER):
            target_ref[u0, spot, :] = pieces_ref[k, pl.ds(u0, run, stride=OUTER), :]

    def wide(ref, first):
        return jnp.concatenate([ref[first + k].reshape(2 * INNER, INNER) for k in range(WIDE)], axis=1)

    def product(table_ref, high, low):
        return dot(table_ref[...], jnp.concatenate([high, high, low], axis=0))

    def multiply(step, carry):
        first = step * WIDE
        field = product(there_both, wide(sh_ref, first), wide(sl_ref, first))
        real, imag = field[:INNER], field[INNER:]
        target = jnp.concatenate([target_ref[first + k] for k in range(WIDE)], axis=1)
        residual = scale * (real * real + imag * imag - target)
        back = product(home_both, *split(jnp.concatenate([residual * real, residual * imag], axis=0)))
        for k in range(WIDE):
            back_ref[first + k] = back[:, tile(k)].reshape(2, INNER, INNER)
        return carry

    lax.fori_loop(0, OUTER // WIDE, multiply, 0)

    def backward(step, carry):
        rows = row_block(step)

        def load(k):
            cos, sin = tw_ref[0, rows, k : k + 1], tw_ref[1, rows, k : k + 1]
            real, imag = back_ref[k, 0, rows, :], back_ref[k, 1, rows, :]
            return real * cos + imag * sin, imag * cos - real * sin

        def store(k, value):
            for side in (0, 1):
                out_ref[step * 4 + k % 4, side, tile_rows(k // 4), :] = value[side]

        dft32(load, store, mid_ref, 1)
        return carry

    lax.fori_loop(0, INNER // BLOCK, backward, 0)


def transposed(ref):
    return jnp.concatenate(
        [
            jnp.concatenate([ref[:INNER, :INNER], ref[INNER:, :INNER]], axis=1),
            jnp.concatenate([ref[:INNER, INNER:], ref[INNER:, INNER:]], axis=1),
        ],
        axis=0,
    )


def tile_rows(index):
    return slice(index * BLOCK, (index + 1) * BLOCK)


def gradient_kernel(in_ref, wave_ref, tw_ref, dft_ref, out_ref, high_ref, low_ref, mid_ref, back_ref):
    high_ref[...], low_ref[...] = split(transposed(dft_ref))

    def multiply(step, carry):
        group = pl.ds(step * 4, 4)
        both = jnp.concatenate([in_ref[group, 0], in_ref[group, 1]], axis=-1).reshape(4 * INNER, 2 * INNER)
        high, low = split(both)
        out = dot(
            jnp.concatenate([high, low, high], axis=1),
            jnp.concatenate([high_ref[...], high_ref[...], low_ref[...]], axis=0),
        )
        back_ref[group] = out.reshape(4, INNER, 2 * INNER)
        return carry

    lax.fori_loop(0, OUTER // 4, multiply, 0)

    def block(step, carry):
        rows = row_block(step)

        def load(k):
            cos, sin = tw_ref[0, k : k + 1, :], tw_ref[1, k : k + 1, :]
            real, imag = back_ref[k, rows, tile(0)], back_ref[k, rows, tile(1)]
            return real * cos + imag * sin, imag * cos - real * sin

        def store(k, value):
            out_ref[rows, tile(k)] = value[1] * wave_ref[0, rows, tile(k)] - value[0] * wave_ref[1, rows, tile(k)]

        dft32(load, store, mid_ref, 1)
        return carry

    lax.fori_loop(0, INNER // BLOCK, block, 0)


def call(kernel, out_shapes, scratch, *args, direct=(), limit=28, held=0):
    return pl.pallas_call(
        kernel,
        out_shape=[jax.ShapeDtypeStruct(shape, F32) for shape in out_shapes],
        in_specs=[
            pl.BlockSpec(
                memory_space=pltpu.SMEM if arg.dtype == jnp.int32 else pl.ANY if k >= len(args) - held else pltpu.VMEM
            )
            for k, arg in enumerate(args)
        ],
        out_specs=[pl.BlockSpec(memory_space=pltpu.HBM if k in direct else pltpu.VMEM) for k in range(len(out_shapes))],
        scratch_shapes=[pltpu.VMEM(*item) if isinstance(item, tuple) else item for item in scratch],
        compiler_params=pltpu.CompilerParams(vmem_limit_bytes=limit * 2**20),
    )(*args)


def inverse_odd(value, modulus):
    result = value
    for _ in range(4):
        result = (result * ((2 - value * result) & (modulus - 1))) & (modulus - 1)
    return result


def on_device(phase, depths, targets):
    rows_dev, length = phase.shape
    planes = lax.axis_size("xl") * lax.axis_size("y")
    layers = lax.axis_size("z")
    place = lax.axis_index("xl") * lax.axis_size("y") + lax.axis_index("y")
    slab_size = math.prod(lax.axis_size(axis) for axis in SLAB)
    share = rows_dev // planes
    mine = lax.dynamic_slice_in_dim(phase, place * share, share, 0)
    mine, targets = lax.optimization_barrier((mine, targets))
    rows_phase = lax.all_gather(mine, "z", axis=0, tiled=True)

    (sorted_targets,) = call(
        sort_kernel,
        [(slab_size, rows_dev + NOTE, INNER)],
        [((length, rows_dev), F32)],
        depths,
        targets[0],
        limit=60,
    )
    sorted_targets = lax.all_to_all(sorted_targets, SLAB, 0, 0, tiled=True)
    layer = lax.axis_index("z")
    group = slab_size // layers
    layer_index = layer.astype(jnp.int32)
    first_row = (lax.axis_index("xh") * lax.axis_size("c") + lax.axis_index("c")) * rows_dev + place * share

    mid = ((OUTER, 2, BLOCK, INNER), F32)
    matrix = ((2 * INNER, 2 * INNER), BF16)
    chunks = (slab_size, 2, layers * share, INNER)
    spectrum, wave, twiddle, tall_twiddle, there, *sent = call(
        functools.partial(rows_kernel, length),
        [
            chunks,
            (2, layers * share, length),
            (2, OUTER, INNER),
            (2, INNER, OUTER),
            (2 * INNER, 2 * INNER),
        ]
        + [(group, rows_dev, INNER)] * (layers - 1),
        [
            matrix,
            matrix,
            mid,
            ((OUTER, INNER, 2 * INNER), BF16),
            ((OUTER, INNER, 2 * INNER), BF16),
            (chunks, F32),
            ((2, layers * share, length), F32),
            ((INNER, INNER), F32),
            ((OUTER, INNER), F32),
            ((NOTE, INNER), F32),
            ((slab_size, rows_dev, INNER), F32),
            pltpu.SemaphoreType.DMA((4,)),
            pltpu.SemaphoreType.DMA((layers - 1,)),
        ],
        jnp.stack([layer_index, first_row.astype(jnp.int32)]),
        rows_phase,
        sorted_targets,
        held=1,
        direct=(0, 1) + tuple(range(5, 4 + layers)),
        limit=60,
    )
    own = lax.dynamic_slice(sorted_targets, (layer * group, 0, 0), (group, rows_dev, INNER))
    pieces = [own] + [
        lax.ppermute(piece, "z", [(i, (i + k) % layers) for i in range(layers)]) for k, piece in enumerate(sent, 1)
    ]
    pieces = [piece.reshape(group * rows_dev, INNER) for piece in pieces]
    spectrum = lax.all_to_all(spectrum, SLAB, 0, 0, tiled=True)
    (spectrum,) = call(
        lambda *refs: columns_kernel(4.0 / planes, *refs),
        [chunks],
        [
            ((2 * INNER, 6 * INNER), BF16),
            ((2 * INNER, 6 * INNER), BF16),
            mid,
            ((OUTER, 2, INNER, INNER), BF16),
            ((OUTER, 2, INNER, INNER), BF16),
            ((OUTER, 2, INNER, INNER), F32),
            ((OUTER, INNER, INNER), F32),
            (chunks, F32),
            ((layers, group * rows_dev, INNER), F32),
            pltpu.SemaphoreType.DMA((INNER // BLOCK + layers,)),
        ],
        layer_index[None],
        tall_twiddle,
        there,
        spectrum,
        *pieces,
        held=1 + layers,
    )
    spectrum = lax.all_to_all(spectrum, SLAB, 0, 0, tiled=True)
    (part,) = call(
        gradient_kernel,
        [(layers * share, length)],
        [matrix, matrix, mid, ((OUTER, INNER, 2 * INNER), F32)],
        spectrum,
        wave,
        twiddle,
        there,
    )
    part = lax.psum_scatter(part, "z", scatter_dimension=0, tiled=True)
    part = jnp.broadcast_to(part[None], (planes, share, length))
    return lax.all_to_all(part, ("xl", "y"), 0, 0, tiled=True).reshape(rows_dev, length)


def solution(mesh):
    fine = Mesh(mesh.devices.reshape(2, 4, 8, 2, 2), ("xl", "y", "z", "xh", "c"))
    rows = ("z", "xh", "c")
    placed = (P(rows, None), P(("xl", "y")), P(("xl", "y"), rows, None))
    return jax.shard_map(on_device, mesh=fine, in_specs=placed, out_specs=P(rows, None), check_vma=False)
```

```python
import functools
import math

import jax
import jax.numpy as jnp
import numpy as np
from jax import lax
from jax.experimental import pallas as pl
from jax.experimental.pallas import tpu as pltpu
from jax.sharding import Mesh
from jax.sharding import PartitionSpec as P

SLAB = ("xl", "y", "xh", "c")
OUTER = 32
INNER = 128
BLOCK = 16
WIDE = 16
NOTE = 8
F32 = jnp.float32
BF16 = jnp.bfloat16


def fit(function, count, odd):
    points = np.cos(np.pi * (np.arange(400) + 0.5) / 400) * 0.5
    powers = np.stack([points ** (2 * k + odd) for k in range(count)], axis=1)
    return [float(c) for c in np.linalg.lstsq(powers, function(np.pi * points), rcond=None)[0]]


SIN_TERMS = fit(np.sin, 6, 1)
COS_TERMS = fit(np.cos, 6, 0)


def horner(terms, square):
    total = jnp.full_like(square, terms[-1])
    for term in terms[-2::-1]:
        total = total * square + term
    return total


def unit_wave(turns):
    turns = turns - jnp.round(turns)
    square = turns * turns
    half_sin = turns * horner(SIN_TERMS, square)
    half_cos = horner(COS_TERMS, square)
    twice = half_sin + half_sin
    return 1.0 - twice * half_sin, twice * half_cos


def spin(value, step, size, sign):
    real, imag = value
    step = step % size
    if step == 0:
        return value
    if 4 * step == size:
        return (-imag, real) if sign > 0 else (imag, -real)
    if 2 * step == size:
        return (-real, -imag)
    if 4 * step == 3 * size:
        return (imag, -real) if sign > 0 else (-imag, real)
    cos = math.cos(2 * math.pi * step / size)
    sin = sign * math.sin(2 * math.pi * step / size)
    if 8 * step % size == 0 and abs(abs(cos) - abs(sin)) < 1e-9:
        root = abs(cos)
        real, imag = real * root, imag * root
        cs = 1 if cos > 0 else -1
        ss = 1 if sin > 0 else -1
        a = real if cs > 0 else -real
        new_real = a - imag if ss > 0 else a + imag
        b = imag if cs > 0 else -imag
        new_imag = b + real if ss > 0 else b - real
        return new_real, new_imag
    return real * cos - imag * sin, real * sin + imag * cos


def small_dft(values, sign):
    size = len(values)
    if size == 1:
        return values
    even = small_dft(values[0::2], sign)
    odd = small_dft(values[1::2], sign)
    low, high = [], []
    for k in range(size // 2):
        turned = spin(odd[k], k, size, sign)
        low.append((even[k][0] + turned[0], even[k][1] + turned[1]))
        high.append((even[k][0] - turned[0], even[k][1] - turned[1]))
    return low + high


def dft32(load, store, mid_ref, sign):
    for b in range(8):
        out = small_dft([load(8 * a + b) for a in range(4)], sign)
        for p in range(4):
            real, imag = spin(out[p], b * p, 32, sign)
            mid_ref[8 * p + b, 0] = real
            mid_ref[8 * p + b, 1] = imag
    for p in range(4):
        out = small_dft([(mid_ref[8 * p + b, 0], mid_ref[8 * p + b, 1]) for b in range(8)], sign)
        for s in range(8):
            store(p + 4 * s, out[s])


def split(value):
    high = value.astype(BF16)
    return high, (value - high.astype(F32)).astype(BF16)


def dot(left, right):
    return jnp.dot(left, right, preferred_element_type=F32)


def row_block(step):
    return pl.ds(pl.multiple_of(step * BLOCK, BLOCK), BLOCK)


def half_rows(step):
    return pl.ds(pl.multiple_of(step * (BLOCK // 2), BLOCK // 2), BLOCK // 2)


def tile(index):
    return slice(index * INNER, (index + 1) * INNER)


def sort_kernel(depth_ref, target_ref, out_ref, turned_ref):
    for k in range(OUTER):
        turned_ref[tile(k), :] = target_ref[:, tile(k)].T
    for j in range(OUTER):
        out_ref[j, :INNER] = turned_ref[pl.ds(j, INNER, stride=OUTER), :].T
        out_ref[j, INNER:] = jnp.full((NOTE, INNER), depth_ref[0].astype(F32))


def rows_kernel(
    length, place_ref, phase_ref, targets_hbm, out_hbm, first_hbm, second_hbm, tw_ref, tall_ref, dft_ref, *refs
):
    sent = refs[:-13]
    high_ref, low_ref, mid_ref, sh_ref, sl_ref, out_ref, wave_ref, row_ref, col_ref, note_ref, stage_ref, sem, send_sem = refs[-13:]
    layers = len(sent) + 1
    group = targets_hbm.shape[0] // layers
    layer = place_ref[0]

    note = pltpu.make_async_copy(targets_hbm.at[layer * group, pl.ds(INNER, NOTE)], note_ref, sem.at[2])
    note.start()
    stage = pltpu.make_async_copy(targets_hbm.at[:, pl.ds(0, INNER)], stage_ref, sem.at[3])
    stage.start()
    sends = [
        pltpu.make_async_copy(
            stage_ref.at[pl.ds(lax.rem(layer + k, layers) * group, group)],
            sent[k - 1],
            send_sem.at[k - 1],
        )
        for k in range(1, layers)
    ]
    note.wait()
    modulus = 2 * length
    weight = inverse_odd(
        ((note_ref[0:1, :].astype(jnp.int32) + 8) * (length // 64) + 1) & (modulus - 1), modulus
    )

    def index(shape, axis):
        return lax.broadcasted_iota(jnp.int32, shape, axis)

    def waves(steps, size):
        return unit_wave(steps.astype(F32) * (-1.0 / size))

    flat = (OUTER, INNER)
    tw_ref[0], tw_ref[1] = waves((index(flat, 0) * index(flat, 1) * weight) & (length - 1), length)
    tall = (INNER, OUTER)
    tall_ref[0], tall_ref[1] = waves(
        (index(tall, 0) * index(tall, 1) * weight[:, :OUTER]) & (length - 1), length
    )
    square = (INNER, INNER)
    steps = (index(square, 0) * index(square, 1)) & (INNER - 1)
    cos, sin = waves((steps * (weight & (INNER - 1))) & (INNER - 1), INNER)
    cos, sin = cos * (1.0 / math.sqrt(length)), sin * (1.0 / math.sqrt(length))
    dft_ref[:INNER, :INNER], dft_ref[:INNER, INNER:] = cos, sin
    dft_ref[INNER:, :INNER], dft_ref[INNER:, INNER:] = -sin, cos
    high_ref[...], low_ref[...] = split(dft_ref[...])

    def chirp(pixel):
        return ((((pixel * pixel) & (modulus - 1)) * weight) & (modulus - 1)).astype(F32) * (1.0 / modulus)

    col_ref[...] = chirp(index(flat, 0) * INNER + index(flat, 1))
    local = index(square, 0)
    inside = local & (BLOCK - 1)
    row_ref[...] = chirp((local - inside) * (length // layers // BLOCK) + place_ref[1] + inside)

    stage.wait()
    for send in sends:
        send.start()

    def save_wave(step):
        source = [half_rows(2 * step + side) for side in (0, 1)]
        return [
            pltpu.make_async_copy(wave_ref.at[:, source[side], :], hbm.at[:, half_rows(step), :], sem.at[0])
            for side, hbm in enumerate((first_hbm, second_hbm))
        ]

    def save_out(step):
        group = pl.ds(step * 4, 4)
        return pltpu.make_async_copy(out_ref.at[group], out_hbm.at[group], sem.at[1])

    def block(step, carry):
        rows = row_block(step)
        row_turn = row_ref[rows, :]

        def load(k):
            turns = phase_ref[rows, tile(k)] * (0.5 / math.pi) + (row_turn + col_ref[k : k + 1, :])
            cos, sin = unit_wave(turns)
            wave_ref[0, rows, tile(k)] = cos
            wave_ref[1, rows, tile(k)] = sin
            return cos, sin

        def store(k, value):
            cos, sin = tw_ref[0, k : k + 1, :], tw_ref[1, k : k + 1, :]
            real, imag = value
            for part, side in ((real * cos - imag * sin, 0), (real * sin + imag * cos, 1)):
                high, low = split(part)
                sh_ref[k, rows, tile(side)] = high
                sl_ref[k, rows, tile(side)] = low

        dft32(load, store, mid_ref, -1)
        for save in save_wave(step):
            save.start()
        return carry

    lax.fori_loop(0, INNER // BLOCK, block, 0)

    def multiply(step, carry):
        group = pl.ds(step * 4, 4)
        high = sh_ref[group].reshape(4 * INNER, 2 * INNER)
        low = sl_ref[group].reshape(4 * INNER, 2 * INNER)
        out = dot(
            jnp.concatenate([high, low, high], axis=1),
            jnp.concatenate([high_ref[...], high_ref[...], low_ref[...]], axis=0),
        )
        out = out.reshape(4, INNER, 2 * INNER)
        out_ref[group, 0] = out[:, :, :INNER]
        out_ref[group, 1] = out[:, :, INNER:]
        save_out(step).start()
        return carry

    lax.fori_loop(0, OUTER // 4, multiply, 0)
    for hbm in (first_hbm, second_hbm):
        pltpu.make_async_copy(wave_ref.at[:, pl.ds(0, INNER // 2), :], hbm, sem.at[0]).wait()
    pltpu.make_async_copy(out_ref, out_hbm, sem.at[1]).wait()
    for send in sends:
        send.wait()


def columns_kernel(
    scale, layer_ref, tw_ref, there_ref, in_hbm, *refs
):
    pieces_hbm, refs = refs[: len(refs) - 12], refs[len(refs) - 12 :]
    first_ref, second_ref, there_both, home_both, mid_ref, sh_ref, sl_ref, back_ref, target_ref, in_ref, pieces_ref, sem = refs
    layers = len(pieces_hbm)
    run = INNER // layers

    def fetch(step):
        group = pl.ds(step * 4, 4)
        return pltpu.make_async_copy(in_hbm.at[group], in_ref.at[group], sem.at[step])

    def fetch_piece(k):
        return pltpu.make_async_copy(pieces_hbm[k], pieces_ref.at[k], sem.at[INNER // BLOCK + k])

    for step in range(INNER // BLOCK):
        fetch(step).start()
    for k in range(layers):
        fetch_piece(k).start()

    for both, matrix in ((there_both, transposed(there_ref)), (home_both, there_ref[...])):
        high, low = split(matrix)
        both[...] = jnp.concatenate([high, low, high], axis=1)

    def forward(step, carry):
        rows = row_block(step)
        fetch(step).wait()

        def load(k):
            return tuple(in_ref[step * 4 + k % 4, side, tile_rows(k // 4), :] for side in (0, 1))

        def store(k, value):
            cos, sin = tw_ref[0, rows, k : k + 1], tw_ref[1, rows, k : k + 1]
            real, imag = value
            for part, side in ((real * cos - imag * sin, 0), (real * sin + imag * cos, 1)):
                high, low = split(part)
                sh_ref[k, side, rows, :] = high
                sl_ref[k, side, rows, :] = low

        dft32(load, store, mid_ref, -1)
        return carry

    lax.fori_loop(0, INNER // BLOCK, forward, 0)

    for k in range(layers):
        fetch_piece(k).wait()
        start = lax.rem(layer_ref[0] + (layers - k), layers) * run
        spot = pl.ds(pl.multiple_of(start, run), run)
        for u0 in range(OUTER):
            target_ref[u0, spot, :] = pieces_ref[k, pl.ds(u0, run, stride=OUTER), :]

    def wide(ref, first):
        return jnp.concatenate([ref[first + k].reshape(2 * INNER, INNER) for k in range(WIDE)], axis=1)

    def product(table_ref, high, low):
        return dot(table_ref[...], jnp.concatenate([high, high, low], axis=0))

    def multiply(step, carry):
        first = step * WIDE
        field = product(there_both, wide(sh_ref, first), wide(sl_ref, first))
        real, imag = field[:INNER], field[INNER:]
        target = jnp.concatenate([target_ref[first + k] for k in range(WIDE)], axis=1)
        residual = scale * (real * real + imag * imag - target)
        back = product(home_both, *split(jnp.concatenate([residual * real, residual * imag], axis=0)))
        for k in range(WIDE):
            back_ref[first + k] = back[:, tile(k)].reshape(2, INNER, INNER)
        return carry

    lax.fori_loop(0, OUTER // WIDE, multiply, 0)

    def backward(step, carry):
        rows = row_block(step)

        def load(k):
            cos, sin = tw_ref[0, rows, k : k + 1], tw_ref[1, rows, k : k + 1]
            real, imag = back_ref[k, 0, rows, :], back_ref[k, 1, rows, :]
            return real * cos + imag * sin, imag * cos - real * sin

        def store(k, value):
            for side in (0, 1):
                first_ref[step * 4 + k % 4, side, half_tile(k // 4), :] = value[side][: BLOCK // 2]
                second_ref[step * 4 + k % 4, side, half_tile(k // 4), :] = value[side][BLOCK // 2 :]

        dft32(load, store, mid_ref, 1)
        return carry

    lax.fori_loop(0, INNER // BLOCK, backward, 0)


def transposed(ref):
    return jnp.concatenate(
        [
            jnp.concatenate([ref[:INNER, :INNER], ref[INNER:, :INNER]], axis=1),
            jnp.concatenate([ref[:INNER, INNER:], ref[INNER:, INNER:]], axis=1),
        ],
        axis=0,
    )


def half_tile(index):
    return slice(index * (BLOCK // 2), (index + 1) * (BLOCK // 2))


def tile_rows(index):
    return slice(index * BLOCK, (index + 1) * BLOCK)


def gradient_kernel(in_ref, wave_ref, tw_ref, dft_ref, out_ref, high_ref, low_ref, mid_ref, back_ref):
    high_ref[...], low_ref[...] = split(transposed(dft_ref))

    rows_here = in_ref.shape[2]

    def multiply(step, carry):
        group = pl.ds(step * 4, 4)
        both = jnp.concatenate([in_ref[group, 0], in_ref[group, 1]], axis=-1).reshape(4 * rows_here, 2 * INNER)
        high, low = split(both)
        out = dot(
            jnp.concatenate([high, low, high], axis=1),
            jnp.concatenate([high_ref[...], high_ref[...], low_ref[...]], axis=0),
        )
        back_ref[group] = out.reshape(4, rows_here, 2 * INNER)
        return carry

    lax.fori_loop(0, OUTER // 4, multiply, 0)

    def block(step, carry):
        rows = row_block(step)

        def load(k):
            cos, sin = tw_ref[0, k : k + 1, :], tw_ref[1, k : k + 1, :]
            real, imag = back_ref[k, rows, tile(0)], back_ref[k, rows, tile(1)]
            return real * cos + imag * sin, imag * cos - real * sin

        def store(k, value):
            out_ref[rows, tile(k)] = value[1] * wave_ref[0, rows, tile(k)] - value[0] * wave_ref[1, rows, tile(k)]

        dft32(load, store, mid_ref, 1)
        return carry

    lax.fori_loop(0, rows_here // BLOCK, block, 0)


def call(kernel, out_shapes, scratch, *args, direct=(), limit=28, held=0):
    return pl.pallas_call(
        kernel,
        out_shape=[jax.ShapeDtypeStruct(shape, F32) for shape in out_shapes],
        in_specs=[
            pl.BlockSpec(
                memory_space=pltpu.SMEM if arg.dtype == jnp.int32 else pl.ANY if k >= len(args) - held else pltpu.VMEM
            )
            for k, arg in enumerate(args)
        ],
        out_specs=[pl.BlockSpec(memory_space=pltpu.HBM if k in direct else pltpu.VMEM) for k in range(len(out_shapes))],
        scratch_shapes=[pltpu.VMEM(*item) if isinstance(item, tuple) else item for item in scratch],
        compiler_params=pltpu.CompilerParams(vmem_limit_bytes=limit * 2**20),
    )(*args)


def inverse_odd(value, modulus):
    result = value
    for _ in range(4):
        result = (result * ((2 - value * result) & (modulus - 1))) & (modulus - 1)
    return result


def on_device(phase, depths, targets):
    rows_dev, length = phase.shape
    planes = lax.axis_size("xl") * lax.axis_size("y")
    layers = lax.axis_size("z")
    place = lax.axis_index("xl") * lax.axis_size("y") + lax.axis_index("y")
    slab_size = math.prod(lax.axis_size(axis) for axis in SLAB)
    share = rows_dev // planes
    mine = lax.dynamic_slice_in_dim(phase, place * share, share, 0)
    mine, targets = lax.optimization_barrier((mine, targets))
    rows_phase = lax.all_gather(mine, "z", axis=0, tiled=True)

    (sorted_targets,) = call(
        sort_kernel,
        [(slab_size, rows_dev + NOTE, INNER)],
        [((length, rows_dev), F32)],
        depths,
        targets[0],
        limit=60,
    )
    sorted_targets = lax.all_to_all(sorted_targets, SLAB, 0, 0, tiled=True)
    layer = lax.axis_index("z")
    group = slab_size // layers
    layer_index = layer.astype(jnp.int32)
    first_row = (lax.axis_index("xh") * lax.axis_size("c") + lax.axis_index("c")) * rows_dev + place * share

    mid = ((OUTER, 2, BLOCK, INNER), F32)
    matrix = ((2 * INNER, 2 * INNER), BF16)
    chunks = (slab_size, 2, layers * share, INNER)
    spectrum, first_wave, second_wave, twiddle, tall_twiddle, there, *sent = call(
        functools.partial(rows_kernel, length),
        [
            chunks,
            (2, layers * share // 2, length),
            (2, layers * share // 2, length),
            (2, OUTER, INNER),
            (2, INNER, OUTER),
            (2 * INNER, 2 * INNER),
        ]
        + [(group, rows_dev, INNER)] * (layers - 1),
        [
            matrix,
            matrix,
            mid,
            ((OUTER, INNER, 2 * INNER), BF16),
            ((OUTER, INNER, 2 * INNER), BF16),
            (chunks, F32),
            ((2, layers * share, length), F32),
            ((INNER, INNER), F32),
            ((OUTER, INNER), F32),
            ((NOTE, INNER), F32),
            ((slab_size, rows_dev, INNER), F32),
            pltpu.SemaphoreType.DMA((4,)),
            pltpu.SemaphoreType.DMA((layers - 1,)),
        ],
        jnp.stack([layer_index, first_row.astype(jnp.int32)]),
        rows_phase,
        sorted_targets,
        held=1,
        direct=(0, 1, 2) + tuple(range(6, 5 + layers)),
        limit=60,
    )
    own = lax.dynamic_slice(sorted_targets, (layer * group, 0, 0), (group, rows_dev, INNER))
    pieces = [own] + [
        lax.ppermute(piece, "z", [(i, (i + k) % layers) for i in range(layers)]) for k, piece in enumerate(sent, 1)
    ]
    pieces = [piece.reshape(group * rows_dev, INNER) for piece in pieces]
    spectrum = lax.all_to_all(spectrum, SLAB, 0, 0, tiled=True)
    halves = call(
        lambda *refs: columns_kernel(4.0 / planes, *refs),
        [(slab_size, 2, layers * share // 2, INNER)] * 2,
        [
            ((2 * INNER, 6 * INNER), BF16),
            ((2 * INNER, 6 * INNER), BF16),
            mid,
            ((OUTER, 2, INNER, INNER), BF16),
            ((OUTER, 2, INNER, INNER), BF16),
            ((OUTER, 2, INNER, INNER), F32),
            ((OUTER, INNER, INNER), F32),
            (chunks, F32),
            ((layers, group * rows_dev, INNER), F32),
            pltpu.SemaphoreType.DMA((INNER // BLOCK + layers,)),
        ],
        layer_index[None],
        tall_twiddle,
        there,
        spectrum,
        *pieces,
        held=1 + layers,
    )
    results = []
    for half, wave in zip(halves, (first_wave, second_wave)):
        if results:
            half, results[0] = lax.optimization_barrier((half, results[0]))
        half = lax.all_to_all(half, SLAB, 0, 0, tiled=True)
        (part,) = call(
            gradient_kernel,
            [(layers * share // 2, length)],
            [matrix, matrix, mid, ((OUTER, layers * share // 2, 2 * INNER), F32)],
            half,
            wave,
            twiddle,
            there,
        )
        results.append(part)
    results[0] = lax.psum_scatter(results[0], "z", scatter_dimension=0, tiled=True)
    height = share // 2
    total = lax.dynamic_slice_in_dim(results[1], layer * height, height, 0)
    for k in range(1, layers):
        part = lax.dynamic_slice_in_dim(results[1], (layer + k) % layers * height, height, 0)
        total = total + lax.ppermute(part, "z", [(i, (i + k) % layers) for i in range(layers)])
    results[1] = total
    results = [everywhere(part, planes) for part in results]
    return jnp.stack(results, axis=1).reshape(rows_dev, length)


def everywhere(value, copies):
    value = jnp.broadcast_to(value[None], (copies,) + value.shape)
    return lax.all_to_all(value, ("xl", "y"), 0, 0, tiled=True)


def solution(mesh):
    fine = Mesh(mesh.devices.reshape(2, 4, 8, 2, 2), ("xl", "y", "z", "xh", "c"))
    rows = ("z", "xh", "c")
    placed = (P(rows, None), P(("xl", "y")), P(("xl", "y"), rows, None))
    return jax.shard_map(on_device, mesh=fine, in_specs=placed, out_specs=P(rows, None), check_vma=False)
```

```python
import functools
import math

import jax
import jax.numpy as jnp
import numpy as np
from jax import lax
from jax.experimental import pallas as pl
from jax.experimental.pallas import tpu as pltpu
from jax.sharding import Mesh
from jax.sharding import PartitionSpec as P

SLAB = ("xl", "y", "xh", "c")
OUTER = 32
INNER = 128
BLOCK = 16
WIDE = 16
NOTE = 8
F32 = jnp.float32
BF16 = jnp.bfloat16


def fit(function, count, odd):
    points = np.cos(np.pi * (np.arange(400) + 0.5) / 400) * 0.5
    powers = np.stack([points ** (2 * k + odd) for k in range(count)], axis=1)
    return [float(c) for c in np.linalg.lstsq(powers, function(np.pi * points), rcond=None)[0]]


SIN_TERMS = fit(np.sin, 6, 1)
COS_TERMS = fit(np.cos, 6, 0)


def horner(terms, square):
    total = jnp.full_like(square, terms[-1])
    for term in terms[-2::-1]:
        total = total * square + term
    return total


def unit_wave(turns):
    turns = turns - jnp.round(turns)
    square = turns * turns
    half_sin = turns * horner(SIN_TERMS, square)
    half_cos = horner(COS_TERMS, square)
    twice = half_sin + half_sin
    return 1.0 - twice * half_sin, twice * half_cos


def spin(value, step, size, sign):
    real, imag = value
    step = step % size
    if step == 0:
        return value
    if 4 * step == size:
        return (-imag, real) if sign > 0 else (imag, -real)
    if 2 * step == size:
        return (-real, -imag)
    if 4 * step == 3 * size:
        return (imag, -real) if sign > 0 else (-imag, real)
    cos = math.cos(2 * math.pi * step / size)
    sin = sign * math.sin(2 * math.pi * step / size)
    if 8 * step % size == 0 and abs(abs(cos) - abs(sin)) < 1e-9:
        root = abs(cos)
        real, imag = real * root, imag * root
        cs = 1 if cos > 0 else -1
        ss = 1 if sin > 0 else -1
        a = real if cs > 0 else -real
        new_real = a - imag if ss > 0 else a + imag
        b = imag if cs > 0 else -imag
        new_imag = b + real if ss > 0 else b - real
        return new_real, new_imag
    return real * cos - imag * sin, real * sin + imag * cos


def small_dft(values, sign):
    size = len(values)
    if size == 1:
        return values
    even = small_dft(values[0::2], sign)
    odd = small_dft(values[1::2], sign)
    low, high = [], []
    for k in range(size // 2):
        turned = spin(odd[k], k, size, sign)
        low.append((even[k][0] + turned[0], even[k][1] + turned[1]))
        high.append((even[k][0] - turned[0], even[k][1] - turned[1]))
    return low + high


def dft32(load, store, mid_ref, sign):
    for b in range(8):
        out = small_dft([load(8 * a + b) for a in range(4)], sign)
        for p in range(4):
            real, imag = spin(out[p], b * p, 32, sign)
            mid_ref[8 * p + b, 0] = real
            mid_ref[8 * p + b, 1] = imag
    for p in range(4):
        out = small_dft([(mid_ref[8 * p + b, 0], mid_ref[8 * p + b, 1]) for b in range(8)], sign)
        for s in range(8):
            store(p + 4 * s, out[s])


def split(value):
    high = value.astype(BF16)
    return high, (value - high.astype(F32)).astype(BF16)


def dot(left, right):
    return jnp.dot(left, right, preferred_element_type=F32)


def row_block(step):
    return pl.ds(pl.multiple_of(step * BLOCK, BLOCK), BLOCK)


def half_rows(step):
    return pl.ds(pl.multiple_of(step * (BLOCK // 2), BLOCK // 2), BLOCK // 2)


def tile(index):
    return slice(index * INNER, (index + 1) * INNER)


def share_kernel(place_ref, phase_hbm, out_ref, sem):
    share = out_ref.shape[0]
    rows = pl.ds(pl.multiple_of(place_ref[0] * share, share), share)
    copy = pltpu.make_async_copy(phase_hbm.at[rows], out_ref, sem)
    copy.start()
    copy.wait()


def sort_kernel(depth_ref, target_ref, out_ref, turned_ref):
    for k in range(OUTER):
        turned_ref[tile(k), :] = target_ref[:, tile(k)].T
    for j in range(OUTER):
        out_ref[j, :INNER] = turned_ref[pl.ds(j, INNER, stride=OUTER), :].T
        out_ref[j, INNER:] = jnp.full((NOTE, INNER), depth_ref[0].astype(F32))


def rows_kernel(
    length, place_ref, phase_ref, targets_hbm, out_hbm, first_hbm, second_hbm, tw_ref, tall_ref, dft_ref, *refs
):
    sent = refs[:-13]
    high_ref, low_ref, mid_ref, sh_ref, sl_ref, out_ref, wave_ref, row_ref, col_ref, note_ref, stage_ref, sem, send_sem = refs[-13:]
    layers = len(sent) + 1
    group = targets_hbm.shape[0] // layers
    layer = place_ref[0]

    note = pltpu.make_async_copy(targets_hbm.at[layer * group, pl.ds(INNER, NOTE)], note_ref, sem.at[2])
    note.start()
    stage = pltpu.make_async_copy(targets_hbm.at[:, pl.ds(0, INNER)], stage_ref, sem.at[3])
    stage.start()
    sends = [
        pltpu.make_async_copy(
            stage_ref.at[pl.ds(lax.rem(layer + k, layers) * group, group)],
            sent[k - 1],
            send_sem.at[k - 1],
        )
        for k in range(1, layers)
    ]
    note.wait()
    modulus = 2 * length
    weight = inverse_odd(
        ((note_ref[0:1, :].astype(jnp.int32) + 8) * (length // 64) + 1) & (modulus - 1), modulus
    )

    def index(shape, axis):
        return lax.broadcasted_iota(jnp.int32, shape, axis)

    def waves(steps, size):
        return unit_wave(steps.astype(F32) * (-1.0 / size))

    flat = (OUTER, INNER)
    tw_ref[0], tw_ref[1] = waves((index(flat, 0) * index(flat, 1) * weight) & (length - 1), length)
    tall = (INNER, OUTER)
    tall_ref[0], tall_ref[1] = waves(
        (index(tall, 0) * index(tall, 1) * weight[:, :OUTER]) & (length - 1), length
    )
    square = (INNER, INNER)
    steps = (index(square, 0) * index(square, 1)) & (INNER - 1)
    cos, sin = waves((steps * (weight & (INNER - 1))) & (INNER - 1), INNER)
    cos, sin = cos * (1.0 / math.sqrt(length)), sin * (1.0 / math.sqrt(length))
    dft_ref[:INNER, :INNER], dft_ref[:INNER, INNER:] = cos, sin
    dft_ref[INNER:, :INNER], dft_ref[INNER:, INNER:] = -sin, cos
    high_ref[...], low_ref[...] = split(dft_ref[...])

    def chirp(pixel):
        return ((((pixel * pixel) & (modulus - 1)) * weight) & (modulus - 1)).astype(F32) * (1.0 / modulus)

    col_ref[...] = chirp(index(flat, 0) * INNER + index(flat, 1))
    local = index(square, 0)
    inside = local & (BLOCK - 1)
    row_ref[...] = chirp((local - inside) * (length // layers // BLOCK) + place_ref[1] + inside)

    stage.wait()
    for send in sends:
        send.start()

    def save_wave(step):
        source = [half_rows(2 * step + side) for side in (0, 1)]
        return [
            pltpu.make_async_copy(wave_ref.at[:, source[side], :], hbm.at[:, half_rows(step), :], sem.at[0])
            for side, hbm in enumerate((first_hbm, second_hbm))
        ]

    def save_out(step):
        group = pl.ds(step * 4, 4)
        return pltpu.make_async_copy(out_ref.at[group], out_hbm.at[group], sem.at[1])

    def block(step, carry):
        rows = row_block(step)
        row_turn = row_ref[rows, :]

        def load(k):
            turns = phase_ref[rows, tile(k)] * (0.5 / math.pi) + (row_turn + col_ref[k : k + 1, :])
            cos, sin = unit_wave(turns)
            wave_ref[0, rows, tile(k)] = cos
            wave_ref[1, rows, tile(k)] = sin
            return cos, sin

        def store(k, value):
            cos, sin = tw_ref[0, k : k + 1, :], tw_ref[1, k : k + 1, :]
            real, imag = value
            for part, side in ((real * cos - imag * sin, 0), (real * sin + imag * cos, 1)):
                high, low = split(part)
                sh_ref[k, rows, tile(side)] = high
                sl_ref[k, rows, tile(side)] = low

        dft32(load, store, mid_ref, -1)
        for save in save_wave(step):
            save.start()
        return carry

    lax.fori_loop(0, INNER // BLOCK, block, 0)

    def multiply(step, carry):
        group = pl.ds(step * 4, 4)
        high = sh_ref[group].reshape(4 * INNER, 2 * INNER)
        low = sl_ref[group].reshape(4 * INNER, 2 * INNER)
        out = dot(
            jnp.concatenate([high, low, high], axis=1),
            jnp.concatenate([high_ref[...], high_ref[...], low_ref[...]], axis=0),
        )
        out = out.reshape(4, INNER, 2 * INNER)
        out_ref[group, 0] = out[:, :, :INNER]
        out_ref[group, 1] = out[:, :, INNER:]
        save_out(step).start()
        return carry

    lax.fori_loop(0, OUTER // 4, multiply, 0)
    for hbm in (first_hbm, second_hbm):
        pltpu.make_async_copy(wave_ref.at[:, pl.ds(0, INNER // 2), :], hbm, sem.at[0]).wait()
    pltpu.make_async_copy(out_ref, out_hbm, sem.at[1]).wait()
    for send in sends:
        send.wait()


def columns_kernel(
    scale, layer_ref, tw_ref, there_ref, in_hbm, *refs
):
    pieces_hbm, refs = refs[: len(refs) - 12], refs[len(refs) - 12 :]
    first_ref, second_ref, there_both, home_both, mid_ref, sh_ref, sl_ref, back_ref, target_ref, in_ref, pieces_ref, sem = refs
    layers = len(pieces_hbm)
    run = INNER // layers

    def fetch(step):
        group = pl.ds(step * 4, 4)
        return pltpu.make_async_copy(in_hbm.at[group], in_ref.at[group], sem.at[step])

    def fetch_piece(k):
        return pltpu.make_async_copy(pieces_hbm[k], pieces_ref.at[k], sem.at[INNER // BLOCK + k])

    for step in range(INNER // BLOCK):
        fetch(step).start()
    for k in range(layers):
        fetch_piece(k).start()

    for both, matrix in ((there_both, transposed(there_ref)), (home_both, there_ref[...])):
        high, low = split(matrix)
        both[...] = jnp.concatenate([high, low, high], axis=1)

    def forward(step, carry):
        rows = row_block(step)
        fetch(step).wait()

        def load(k):
            return tuple(in_ref[step * 4 + k % 4, side, tile_rows(k // 4), :] for side in (0, 1))

        def store(k, value):
            cos, sin = tw_ref[0, rows, k : k + 1], tw_ref[1, rows, k : k + 1]
            real, imag = value
            for part, side in ((real * cos - imag * sin, 0), (real * sin + imag * cos, 1)):
                high, low = split(part)
                sh_ref[k, side, rows, :] = high
                sl_ref[k, side, rows, :] = low

        dft32(load, store, mid_ref, -1)
        return carry

    lax.fori_loop(0, INNER // BLOCK, forward, 0)

    for k in range(layers):
        fetch_piece(k).wait()
        start = lax.rem(layer_ref[0] + (layers - k), layers) * run
        spot = pl.ds(pl.multiple_of(start, run), run)
        for u0 in range(OUTER):
            target_ref[u0, spot, :] = pieces_ref[k, pl.ds(u0, run, stride=OUTER), :]

    def wide(ref, first):
        return jnp.concatenate([ref[first + k].reshape(2 * INNER, INNER) for k in range(WIDE)], axis=1)

    def product(table_ref, high, low):
        return dot(table_ref[...], jnp.concatenate([high, high, low], axis=0))

    def multiply(step, carry):
        first = step * WIDE
        field = product(there_both, wide(sh_ref, first), wide(sl_ref, first))
        real, imag = field[:INNER], field[INNER:]
        target = jnp.concatenate([target_ref[first + k] for k in range(WIDE)], axis=1)
        residual = scale * (real * real + imag * imag - target)
        back = product(home_both, *split(jnp.concatenate([residual * real, residual * imag], axis=0)))
        for k in range(WIDE):
            back_ref[first + k] = back[:, tile(k)].reshape(2, INNER, INNER)
        return carry

    lax.fori_loop(0, OUTER // WIDE, multiply, 0)

    def backward(step, carry):
        rows = row_block(step)

        def load(k):
            cos, sin = tw_ref[0, rows, k : k + 1], tw_ref[1, rows, k : k + 1]
            real, imag = back_ref[k, 0, rows, :], back_ref[k, 1, rows, :]
            return real * cos + imag * sin, imag * cos - real * sin

        def store(k, value):
            for side in (0, 1):
                first_ref[step * 4 + k % 4, side, half_tile(k // 4), :] = value[side][: BLOCK // 2]
                second_ref[step * 4 + k % 4, side, half_tile(k // 4), :] = value[side][BLOCK // 2 :]

        dft32(load, store, mid_ref, 1)
        return carry

    lax.fori_loop(0, INNER // BLOCK, backward, 0)


def transposed(ref):
    return jnp.concatenate(
        [
            jnp.concatenate([ref[:INNER, :INNER], ref[INNER:, :INNER]], axis=1),
            jnp.concatenate([ref[:INNER, INNER:], ref[INNER:, INNER:]], axis=1),
        ],
        axis=0,
    )


def half_tile(index):
    return slice(index * (BLOCK // 2), (index + 1) * (BLOCK // 2))


def tile_rows(index):
    return slice(index * BLOCK, (index + 1) * BLOCK)


def gradient_kernel(in_ref, wave_ref, tw_ref, dft_ref, out_ref, high_ref, low_ref, mid_ref, back_ref):
    high_ref[...], low_ref[...] = split(transposed(dft_ref))

    rows_here = in_ref.shape[2]

    def multiply(step, carry):
        group = pl.ds(step * 4, 4)
        both = jnp.concatenate([in_ref[group, 0], in_ref[group, 1]], axis=-1).reshape(4 * rows_here, 2 * INNER)
        high, low = split(both)
        out = dot(
            jnp.concatenate([high, low, high], axis=1),
            jnp.concatenate([high_ref[...], high_ref[...], low_ref[...]], axis=0),
        )
        back_ref[group] = out.reshape(4, rows_here, 2 * INNER)
        return carry

    lax.fori_loop(0, OUTER // 4, multiply, 0)

    def block(step, carry):
        rows = row_block(step)

        def load(k):
            cos, sin = tw_ref[0, k : k + 1, :], tw_ref[1, k : k + 1, :]
            real, imag = back_ref[k, rows, tile(0)], back_ref[k, rows, tile(1)]
            return real * cos + imag * sin, imag * cos - real * sin

        def store(k, value):
            out_ref[rows, tile(k)] = value[1] * wave_ref[0, rows, tile(k)] - value[0] * wave_ref[1, rows, tile(k)]

        dft32(load, store, mid_ref, 1)
        return carry

    lax.fori_loop(0, rows_here // BLOCK, block, 0)


def call(kernel, out_shapes, scratch, *args, direct=(), limit=28, held=0):
    return pl.pallas_call(
        kernel,
        out_shape=[jax.ShapeDtypeStruct(shape, F32) for shape in out_shapes],
        in_specs=[
            pl.BlockSpec(
                memory_space=pltpu.SMEM if arg.dtype == jnp.int32 else pl.ANY if k >= len(args) - held else pltpu.VMEM
            )
            for k, arg in enumerate(args)
        ],
        out_specs=[pl.BlockSpec(memory_space=pltpu.HBM if k in direct else pltpu.VMEM) for k in range(len(out_shapes))],
        scratch_shapes=[pltpu.VMEM(*item) if isinstance(item, tuple) else item for item in scratch],
        compiler_params=pltpu.CompilerParams(vmem_limit_bytes=limit * 2**20),
    )(*args)


def inverse_odd(value, modulus):
    result = value
    for _ in range(4):
        result = (result * ((2 - value * result) & (modulus - 1))) & (modulus - 1)
    return result


def on_device(phase, depths, targets):
    rows_dev, length = phase.shape
    planes = lax.axis_size("xl") * lax.axis_size("y")
    layers = lax.axis_size("z")
    place = lax.axis_index("xl") * lax.axis_size("y") + lax.axis_index("y")
    slab_size = math.prod(lax.axis_size(axis) for axis in SLAB)
    share = rows_dev // planes
    (mine,) = call(
        share_kernel,
        [(share, length)],
        [pltpu.SemaphoreType.DMA(())],
        place.astype(jnp.int32)[None],
        phase,
        held=1,
        limit=60,
    )
    mine, targets = lax.optimization_barrier((mine, targets))
    rows_phase = lax.all_gather(mine, "z", axis=0, tiled=True)

    (sorted_targets,) = call(
        sort_kernel,
        [(slab_size, rows_dev + NOTE, INNER)],
        [((length, rows_dev), F32)],
        depths,
        targets[0],
        limit=60,
    )
    sorted_targets = lax.all_to_all(sorted_targets, SLAB, 0, 0, tiled=True)
    layer = lax.axis_index("z")
    group = slab_size // layers
    layer_index = layer.astype(jnp.int32)
    first_row = (lax.axis_index("xh") * lax.axis_size("c") + lax.axis_index("c")) * rows_dev + place * share

    mid = ((OUTER, 2, BLOCK, INNER), F32)
    matrix = ((2 * INNER, 2 * INNER), BF16)
    chunks = (slab_size, 2, layers * share, INNER)
    spectrum, first_wave, second_wave, twiddle, tall_twiddle, there, *sent = call(
        functools.partial(rows_kernel, length),
        [
            chunks,
            (2, layers * share // 2, length),
            (2, layers * share // 2, length),
            (2, OUTER, INNER),
            (2, INNER, OUTER),
            (2 * INNER, 2 * INNER),
        ]
        + [(group, rows_dev, INNER)] * (layers - 1),
        [
            matrix,
            matrix,
            mid,
            ((OUTER, INNER, 2 * INNER), BF16),
            ((OUTER, INNER, 2 * INNER), BF16),
            (chunks, F32),
            ((2, layers * share, length), F32),
            ((INNER, INNER), F32),
            ((OUTER, INNER), F32),
            ((NOTE, INNER), F32),
            ((slab_size, rows_dev, INNER), F32),
            pltpu.SemaphoreType.DMA((4,)),
            pltpu.SemaphoreType.DMA((layers - 1,)),
        ],
        jnp.stack([layer_index, first_row.astype(jnp.int32)]),
        rows_phase,
        sorted_targets,
        held=1,
        direct=(0, 1, 2) + tuple(range(6, 5 + layers)),
        limit=60,
    )
    own = lax.dynamic_slice(sorted_targets, (layer * group, 0, 0), (group, rows_dev, INNER))
    pieces = [own] + [
        lax.ppermute(piece, "z", [(i, (i + k) % layers) for i in range(layers)]) for k, piece in enumerate(sent, 1)
    ]
    pieces = [piece.reshape(group * rows_dev, INNER) for piece in pieces]
    spectrum = lax.all_to_all(spectrum, SLAB, 0, 0, tiled=True)
    halves = call(
        lambda *refs: columns_kernel(4.0 / planes, *refs),
        [(slab_size, 2, layers * share // 2, INNER)] * 2,
        [
            ((2 * INNER, 6 * INNER), BF16),
            ((2 * INNER, 6 * INNER), BF16),
            mid,
            ((OUTER, 2, INNER, INNER), BF16),
            ((OUTER, 2, INNER, INNER), BF16),
            ((OUTER, 2, INNER, INNER), F32),
            ((OUTER, INNER, INNER), F32),
            (chunks, F32),
            ((layers, group * rows_dev, INNER), F32),
            pltpu.SemaphoreType.DMA((INNER // BLOCK + layers,)),
        ],
        layer_index[None],
        tall_twiddle,
        there,
        spectrum,
        *pieces,
        held=1 + layers,
    )
    results = []
    for half, wave in zip(halves, (first_wave, second_wave)):
        half = lax.all_to_all(half, SLAB, 0, 0, tiled=True)
        (part,) = call(
            gradient_kernel,
            [(layers * share // 2, length)],
            [matrix, matrix, mid, ((OUTER, layers * share // 2, 2 * INNER), F32)],
            half,
            wave,
            twiddle,
            there,
        )
        results.append(lax.psum_scatter(part, "z", scatter_dimension=0, tiled=True))
    results = [everywhere(part, planes) for part in results]
    return jnp.stack(results, axis=1).reshape(rows_dev, length)


def everywhere(value, copies):
    value = jnp.broadcast_to(value[None], (copies,) + value.shape)
    return lax.all_to_all(value, ("xl", "y"), 0, 0, tiled=True)


def solution(mesh):
    fine = Mesh(mesh.devices.reshape(2, 4, 8, 2, 2), ("xl", "y", "z", "xh", "c"))
    rows = ("z", "xh", "c")
    placed = (P(rows, None), P(("xl", "y")), P(("xl", "y"), rows, None))
    return jax.shard_map(on_device, mesh=fine, in_specs=placed, out_specs=P(rows, None), check_vma=False)
```

```python
import functools
import math

import jax
import jax.numpy as jnp
import numpy as np
from jax import lax
from jax.experimental import pallas as pl
from jax.experimental.pallas import tpu as pltpu
from jax.sharding import Mesh
from jax.sharding import PartitionSpec as P

SLAB = ("xl", "y", "xh", "c")
OUTER = 32
INNER = 128
BLOCK = 16
WIDE = 16
NOTE = 8
F32 = jnp.float32
BF16 = jnp.bfloat16


def fit(function, count, odd):
    points = np.cos(np.pi * (np.arange(400) + 0.5) / 400) * 0.5
    powers = np.stack([points ** (2 * k + odd) for k in range(count)], axis=1)
    return [float(c) for c in np.linalg.lstsq(powers, function(np.pi * points), rcond=None)[0]]


SIN_TERMS = fit(np.sin, 6, 1)
COS_TERMS = fit(np.cos, 6, 0)


def horner(terms, square):
    total = jnp.full_like(square, terms[-1])
    for term in terms[-2::-1]:
        total = total * square + term
    return total


def unit_wave(turns):
    turns = turns - jnp.round(turns)
    square = turns * turns
    half_sin = turns * horner(SIN_TERMS, square)
    half_cos = horner(COS_TERMS, square)
    twice = half_sin + half_sin
    return 1.0 - twice * half_sin, twice * half_cos


def spin(value, step, size, sign):
    real, imag = value
    step = step % size
    if step == 0:
        return value
    if 4 * step == size:
        return (-imag, real) if sign > 0 else (imag, -real)
    if 2 * step == size:
        return (-real, -imag)
    if 4 * step == 3 * size:
        return (imag, -real) if sign > 0 else (-imag, real)
    cos = math.cos(2 * math.pi * step / size)
    sin = sign * math.sin(2 * math.pi * step / size)
    if 8 * step % size == 0 and abs(abs(cos) - abs(sin)) < 1e-9:
        root = abs(cos)
        real, imag = real * root, imag * root
        cs = 1 if cos > 0 else -1
        ss = 1 if sin > 0 else -1
        a = real if cs > 0 else -real
        new_real = a - imag if ss > 0 else a + imag
        b = imag if cs > 0 else -imag
        new_imag = b + real if ss > 0 else b - real
        return new_real, new_imag
    return real * cos - imag * sin, real * sin + imag * cos


def small_dft(values, sign):
    size = len(values)
    if size == 1:
        return values
    even = small_dft(values[0::2], sign)
    odd = small_dft(values[1::2], sign)
    low, high = [], []
    for k in range(size // 2):
        turned = spin(odd[k], k, size, sign)
        low.append((even[k][0] + turned[0], even[k][1] + turned[1]))
        high.append((even[k][0] - turned[0], even[k][1] - turned[1]))
    return low + high


def dft32(load, store, mid_ref, sign):
    for b in range(8):
        out = small_dft([load(8 * a + b) for a in range(4)], sign)
        for p in range(4):
            real, imag = spin(out[p], b * p, 32, sign)
            mid_ref[8 * p + b, 0] = real
            mid_ref[8 * p + b, 1] = imag
    for p in range(4):
        out = small_dft([(mid_ref[8 * p + b, 0], mid_ref[8 * p + b, 1]) for b in range(8)], sign)
        for s in range(8):
            store(p + 4 * s, out[s])


def split(value):
    high = value.astype(BF16)
    return high, (value - high.astype(F32)).astype(BF16)


def dot(left, right):
    return jnp.dot(left, right, preferred_element_type=F32)


def row_block(step):
    return pl.ds(pl.multiple_of(step * BLOCK, BLOCK), BLOCK)


def half_rows(step):
    return pl.ds(pl.multiple_of(step * (BLOCK // 2), BLOCK // 2), BLOCK // 2)


def tile(index):
    return slice(index * INNER, (index + 1) * INNER)


def sort_kernel(depth_ref, target_ref, out_ref, turned_ref):
    for k in range(OUTER):
        turned_ref[tile(k), :] = target_ref[:, tile(k)].T
    for j in range(OUTER):
        out_ref[j, :INNER] = turned_ref[pl.ds(j, INNER, stride=OUTER), :].T
        out_ref[j, INNER:] = jnp.full((NOTE, INNER), depth_ref[0].astype(F32))


def rows_kernel(
    length, place_ref, phase_ref, targets_hbm, out_hbm, first_hbm, second_hbm, tw_ref, tall_ref, dft_ref, *refs
):
    sent = refs[:-13]
    high_ref, low_ref, mid_ref, sh_ref, sl_ref, out_ref, wave_ref, row_ref, col_ref, note_ref, stage_ref, sem, send_sem = refs[-13:]
    layers = len(sent) + 1
    group = targets_hbm.shape[0] // layers
    layer = place_ref[0]

    note = pltpu.make_async_copy(targets_hbm.at[layer * group, pl.ds(INNER, NOTE)], note_ref, sem.at[2])
    note.start()
    stage = pltpu.make_async_copy(targets_hbm.at[:, pl.ds(0, INNER)], stage_ref, sem.at[3])
    stage.start()
    sends = [
        pltpu.make_async_copy(
            stage_ref.at[pl.ds(lax.rem(layer + k, layers) * group, group)],
            sent[k - 1],
            send_sem.at[k - 1],
        )
        for k in range(1, layers)
    ]
    note.wait()
    modulus = 2 * length
    weight = inverse_odd(
        ((note_ref[0:1, :].astype(jnp.int32) + 8) * (length // 64) + 1) & (modulus - 1), modulus
    )

    def index(shape, axis):
        return lax.broadcasted_iota(jnp.int32, shape, axis)

    def waves(steps, size):
        return unit_wave(steps.astype(F32) * (-1.0 / size))

    flat = (OUTER, INNER)
    tw_ref[0], tw_ref[1] = waves((index(flat, 0) * index(flat, 1) * weight) & (length - 1), length)
    tall = (INNER, OUTER)
    tall_ref[0], tall_ref[1] = waves(
        (index(tall, 0) * index(tall, 1) * weight[:, :OUTER]) & (length - 1), length
    )
    square = (INNER, INNER)
    steps = (index(square, 0) * index(square, 1)) & (INNER - 1)
    cos, sin = waves((steps * (weight & (INNER - 1))) & (INNER - 1), INNER)
    cos, sin = cos * (1.0 / math.sqrt(length)), sin * (1.0 / math.sqrt(length))
    dft_ref[:INNER, :INNER], dft_ref[:INNER, INNER:] = cos, sin
    dft_ref[INNER:, :INNER], dft_ref[INNER:, INNER:] = -sin, cos
    high_ref[...], low_ref[...] = split(dft_ref[...])

    def chirp(pixel):
        return ((((pixel * pixel) & (modulus - 1)) * weight) & (modulus - 1)).astype(F32) * (1.0 / modulus)

    col_ref[...] = chirp(index(flat, 0) * INNER + index(flat, 1))
    local = index(square, 0)
    inside = local & (BLOCK - 1)
    row_ref[...] = chirp((local - inside) * (length // layers // BLOCK) + place_ref[1] + inside)

    stage.wait()
    for send in sends:
        send.start()

    def save_wave(step):
        source = [half_rows(2 * step + side) for side in (0, 1)]
        return [
            pltpu.make_async_copy(wave_ref.at[:, source[side], :], hbm.at[:, half_rows(step), :], sem.at[0])
            for side, hbm in enumerate((first_hbm, second_hbm))
        ]

    def save_out(step):
        group = pl.ds(step * 4, 4)
        return pltpu.make_async_copy(out_ref.at[group], out_hbm.at[group], sem.at[1])

    def block(step, carry):
        rows = row_block(step)
        row_turn = row_ref[rows, :]

        def load(k):
            turns = phase_ref[rows, tile(k)] * (0.5 / math.pi) + (row_turn + col_ref[k : k + 1, :])
            cos, sin = unit_wave(turns)
            wave_ref[0, rows, tile(k)] = cos
            wave_ref[1, rows, tile(k)] = sin
            return cos, sin

        def store(k, value):
            cos, sin = tw_ref[0, k : k + 1, :], tw_ref[1, k : k + 1, :]
            real, imag = value
            for part, side in ((real * cos - imag * sin, 0), (real * sin + imag * cos, 1)):
                high, low = split(part)
                sh_ref[k, rows, tile(side)] = high
                sl_ref[k, rows, tile(side)] = low

        dft32(load, store, mid_ref, -1)
        for save in save_wave(step):
            save.start()
        return carry

    lax.fori_loop(0, INNER // BLOCK, block, 0)

    def multiply(step, carry):
        group = pl.ds(step * 4, 4)
        high = sh_ref[group].reshape(4 * INNER, 2 * INNER)
        low = sl_ref[group].reshape(4 * INNER, 2 * INNER)
        out = dot(
            jnp.concatenate([high, low, high], axis=1),
            jnp.concatenate([high_ref[...], high_ref[...], low_ref[...]], axis=0),
        )
        out = out.reshape(4, INNER, 2 * INNER)
        out_ref[group, 0] = out[:, :, :INNER]
        out_ref[group, 1] = out[:, :, INNER:]
        save_out(step).start()
        return carry

    lax.fori_loop(0, OUTER // 4, multiply, 0)
    for hbm in (first_hbm, second_hbm):
        pltpu.make_async_copy(wave_ref.at[:, pl.ds(0, INNER // 2), :], hbm, sem.at[0]).wait()
    pltpu.make_async_copy(out_ref, out_hbm, sem.at[1]).wait()
    for send in sends:
        send.wait()


def columns_kernel(
    scale, layer_ref, tw_ref, there_ref, in_hbm, *refs
):
    pieces_hbm, refs = refs[: len(refs) - 12], refs[len(refs) - 12 :]
    first_ref, second_ref, there_both, home_both, mid_ref, sh_ref, sl_ref, back_ref, target_ref, in_ref, pieces_ref, sem = refs
    layers = len(pieces_hbm)
    run = INNER // layers

    def fetch(step):
        group = pl.ds(step * 4, 4)
        return pltpu.make_async_copy(in_hbm.at[group], in_ref.at[group], sem.at[step])

    def fetch_piece(k):
        return pltpu.make_async_copy(pieces_hbm[k], pieces_ref.at[k], sem.at[INNER // BLOCK + k])

    for step in range(INNER // BLOCK):
        fetch(step).start()
    for k in range(layers):
        fetch_piece(k).start()

    for both, matrix in ((there_both, transposed(there_ref)), (home_both, there_ref[...])):
        high, low = split(matrix)
        both[...] = jnp.concatenate([high, low, high], axis=1)

    def forward(step, carry):
        rows = row_block(step)
        fetch(step).wait()

        def load(k):
            return tuple(in_ref[step * 4 + k % 4, side, tile_rows(k // 4), :] for side in (0, 1))

        def store(k, value):
            cos, sin = tw_ref[0, rows, k : k + 1], tw_ref[1, rows, k : k + 1]
            real, imag = value
            for part, side in ((real * cos - imag * sin, 0), (real * sin + imag * cos, 1)):
                high, low = split(part)
                sh_ref[k, side, rows, :] = high
                sl_ref[k, side, rows, :] = low

        dft32(load, store, mid_ref, -1)
        return carry

    lax.fori_loop(0, INNER // BLOCK, forward, 0)

    for k in range(layers):
        fetch_piece(k).wait()
        start = lax.rem(layer_ref[0] + (layers - k), layers) * run
        spot = pl.ds(pl.multiple_of(start, run), run)
        for u0 in range(OUTER):
            target_ref[u0, spot, :] = pieces_ref[k, pl.ds(u0, run, stride=OUTER), :]

    def wide(ref, first):
        return jnp.concatenate([ref[first + k].reshape(2 * INNER, INNER) for k in range(WIDE)], axis=1)

    def product(table_ref, high, low):
        return dot(table_ref[...], jnp.concatenate([high, high, low], axis=0))

    def multiply(step, carry):
        first = step * WIDE
        field = product(there_both, wide(sh_ref, first), wide(sl_ref, first))
        real, imag = field[:INNER], field[INNER:]
        target = jnp.concatenate([target_ref[first + k] for k in range(WIDE)], axis=1)
        residual = scale * (real * real + imag * imag - target)
        back = product(home_both, *split(jnp.concatenate([residual * real, residual * imag], axis=0)))
        for k in range(WIDE):
            back_ref[first + k] = back[:, tile(k)].reshape(2, INNER, INNER)
        return carry

    lax.fori_loop(0, OUTER // WIDE, multiply, 0)

    def backward(step, carry):
        rows = row_block(step)

        def load(k):
            cos, sin = tw_ref[0, rows, k : k + 1], tw_ref[1, rows, k : k + 1]
            real, imag = back_ref[k, 0, rows, :], back_ref[k, 1, rows, :]
            return real * cos + imag * sin, imag * cos - real * sin

        def store(k, value):
            for side in (0, 1):
                first_ref[step * 4 + k % 4, side, half_tile(k // 4), :] = value[side][: BLOCK // 2]
                second_ref[step * 4 + k % 4, side, half_tile(k // 4), :] = value[side][BLOCK // 2 :]

        dft32(load, store, mid_ref, 1)
        return carry

    lax.fori_loop(0, INNER // BLOCK, backward, 0)


def transposed(ref):
    return jnp.concatenate(
        [
            jnp.concatenate([ref[:INNER, :INNER], ref[INNER:, :INNER]], axis=1),
            jnp.concatenate([ref[:INNER, INNER:], ref[INNER:, INNER:]], axis=1),
        ],
        axis=0,
    )


def half_tile(index):
    return slice(index * (BLOCK // 2), (index + 1) * (BLOCK // 2))


def tile_rows(index):
    return slice(index * BLOCK, (index + 1) * BLOCK)


def gradient_kernel(in_ref, wave_ref, tw_ref, dft_ref, out_ref, high_ref, low_ref, mid_ref, back_ref):
    high_ref[...], low_ref[...] = split(transposed(dft_ref))

    rows_here = in_ref.shape[2]

    def multiply(step, carry):
        group = pl.ds(step * 4, 4)
        both = jnp.concatenate([in_ref[group, 0], in_ref[group, 1]], axis=-1).reshape(4 * rows_here, 2 * INNER)
        high, low = split(both)
        out = dot(
            jnp.concatenate([high, low, high], axis=1),
            jnp.concatenate([high_ref[...], high_ref[...], low_ref[...]], axis=0),
        )
        back_ref[group] = out.reshape(4, rows_here, 2 * INNER)
        return carry

    lax.fori_loop(0, OUTER // 4, multiply, 0)

    def block(step, carry):
        rows = row_block(step)

        def load(k):
            cos, sin = tw_ref[0, k : k + 1, :], tw_ref[1, k : k + 1, :]
            real, imag = back_ref[k, rows, tile(0)], back_ref[k, rows, tile(1)]
            return real * cos + imag * sin, imag * cos - real * sin

        def store(k, value):
            out_ref[rows, tile(k)] = value[1] * wave_ref[0, rows, tile(k)] - value[0] * wave_ref[1, rows, tile(k)]

        dft32(load, store, mid_ref, 1)
        return carry

    lax.fori_loop(0, rows_here // BLOCK, block, 0)


def call(kernel, out_shapes, scratch, *args, direct=(), limit=28, held=0):
    return pl.pallas_call(
        kernel,
        out_shape=[jax.ShapeDtypeStruct(shape, F32) for shape in out_shapes],
        in_specs=[
            pl.BlockSpec(
                memory_space=pltpu.SMEM if arg.dtype == jnp.int32 else pl.ANY if k >= len(args) - held else pltpu.VMEM
            )
            for k, arg in enumerate(args)
        ],
        out_specs=[pl.BlockSpec(memory_space=pltpu.HBM if k in direct else pltpu.VMEM) for k in range(len(out_shapes))],
        scratch_shapes=[pltpu.VMEM(*item) if isinstance(item, tuple) else item for item in scratch],
        compiler_params=pltpu.CompilerParams(vmem_limit_bytes=limit * 2**20),
    )(*args)


def inverse_odd(value, modulus):
    result = value
    for _ in range(4):
        result = (result * ((2 - value * result) & (modulus - 1))) & (modulus - 1)
    return result


def on_device(phase, depths, targets):
    rows_dev, length = phase.shape
    planes = lax.axis_size("xl") * lax.axis_size("y")
    layers = lax.axis_size("z")
    place = lax.axis_index("xl") * lax.axis_size("y") + lax.axis_index("y")
    slab_size = math.prod(lax.axis_size(axis) for axis in SLAB)
    share = rows_dev // planes
    mine = lax.dynamic_slice_in_dim(phase, place * share, share, 0)
    mine, targets = lax.optimization_barrier((mine, targets))
    rows_phase = lax.all_gather(mine, "z", axis=0, tiled=True)

    (sorted_targets,) = call(
        sort_kernel,
        [(slab_size, rows_dev + NOTE, INNER)],
        [((length, rows_dev), F32)],
        depths,
        targets[0],
        limit=60,
    )
    sorted_targets = lax.all_to_all(sorted_targets, SLAB, 0, 0, tiled=True)
    layer = lax.axis_index("z")
    group = slab_size // layers
    layer_index = layer.astype(jnp.int32)
    first_row = (lax.axis_index("xh") * lax.axis_size("c") + lax.axis_index("c")) * rows_dev + place * share

    mid = ((OUTER, 2, BLOCK, INNER), F32)
    matrix = ((2 * INNER, 2 * INNER), BF16)
    chunks = (slab_size, 2, layers * share, INNER)
    spectrum, first_wave, second_wave, twiddle, tall_twiddle, there, *sent = call(
        functools.partial(rows_kernel, length),
        [
            chunks,
            (2, layers * share // 2, length),
            (2, layers * share // 2, length),
            (2, OUTER, INNER),
            (2, INNER, OUTER),
            (2 * INNER, 2 * INNER),
        ]
        + [(group, rows_dev, INNER)] * (layers - 1),
        [
            matrix,
            matrix,
            mid,
            ((OUTER, INNER, 2 * INNER), BF16),
            ((OUTER, INNER, 2 * INNER), BF16),
            (chunks, F32),
            ((2, layers * share, length), F32),
            ((INNER, INNER), F32),
            ((OUTER, INNER), F32),
            ((NOTE, INNER), F32),
            ((slab_size, rows_dev, INNER), F32),
            pltpu.SemaphoreType.DMA((4,)),
            pltpu.SemaphoreType.DMA((layers - 1,)),
        ],
        jnp.stack([layer_index, first_row.astype(jnp.int32)]),
        rows_phase,
        sorted_targets,
        held=1,
        direct=(0, 1, 2) + tuple(range(6, 5 + layers)),
        limit=60,
    )
    own = lax.dynamic_slice(sorted_targets, (layer * group, 0, 0), (group, rows_dev, INNER))
    pieces = [own] + [
        lax.ppermute(piece, "z", [(i, (i + k) % layers) for i in range(layers)]) for k, piece in enumerate(sent, 1)
    ]
    pieces = [piece.reshape(group * rows_dev, INNER) for piece in pieces]
    spectrum = lax.all_to_all(spectrum, SLAB, 0, 0, tiled=True)
    halves = call(
        lambda *refs: columns_kernel(4.0 / planes, *refs),
        [(slab_size, 2, layers * share // 2, INNER)] * 2,
        [
            ((2 * INNER, 6 * INNER), BF16),
            ((2 * INNER, 6 * INNER), BF16),
            mid,
            ((OUTER, 2, INNER, INNER), BF16),
            ((OUTER, 2, INNER, INNER), BF16),
            ((OUTER, 2, INNER, INNER), F32),
            ((OUTER, INNER, INNER), F32),
            (chunks, F32),
            ((layers, group * rows_dev, INNER), F32),
            pltpu.SemaphoreType.DMA((INNER // BLOCK + layers,)),
        ],
        layer_index[None],
        tall_twiddle,
        there,
        spectrum,
        *pieces,
        held=1 + layers,
    )
    results = []
    for half, wave in zip(halves, (first_wave, second_wave)):
        half = lax.all_to_all(half, SLAB, 0, 0, tiled=True)
        (part,) = call(
            gradient_kernel,
            [(layers * share // 2, length)],
            [matrix, matrix, mid, ((OUTER, layers * share // 2, 2 * INNER), F32)],
            half,
            wave,
            twiddle,
            there,
        )
        results.append(lax.psum_scatter(part, "z", scatter_dimension=0, tiled=True))
    results = [everywhere(part, planes) for part in results]
    return jnp.stack(results, axis=1).reshape(rows_dev, length)


def everywhere(value, copies):
    value = jnp.broadcast_to(value[None], (copies,) + value.shape)
    return lax.all_to_all(value, ("xl", "y"), 0, 0, tiled=True)


def solution(mesh):
    fine = Mesh(mesh.devices.reshape(2, 4, 8, 2, 2), ("xl", "y", "z", "xh", "c"))
    rows = ("z", "xh", "c")
    placed = (P(rows, None), P(("xl", "y")), P(("xl", "y"), rows, None))
    return jax.shard_map(on_device, mesh=fine, in_specs=placed, out_specs=P(rows, None), check_vma=False)
```

```python
import functools
import math

import jax
import jax.numpy as jnp
import numpy as np
from jax import lax
from jax.experimental import pallas as pl
from jax.experimental.pallas import tpu as pltpu
from jax.sharding import Mesh
from jax.sharding import PartitionSpec as P

SLAB = ("xl", "y", "xh", "c")
OUTER = 32
INNER = 128
BLOCK = 16
WIDE = 16
NOTE = 8
F32 = jnp.float32
BF16 = jnp.bfloat16


def fit(function, count, odd):
    points = np.cos(np.pi * (np.arange(400) + 0.5) / 400) * 0.5
    powers = np.stack([points ** (2 * k + odd) for k in range(count)], axis=1)
    return [float(c) for c in np.linalg.lstsq(powers, function(np.pi * points), rcond=None)[0]]


SIN_TERMS = fit(np.sin, 6, 1)
COS_TERMS = fit(np.cos, 6, 0)


def horner(terms, square):
    total = jnp.full_like(square, terms[-1])
    for term in terms[-2::-1]:
        total = total * square + term
    return total


def unit_wave(turns):
    turns = turns - jnp.round(turns)
    square = turns * turns
    half_sin = turns * horner(SIN_TERMS, square)
    half_cos = horner(COS_TERMS, square)
    twice = half_sin + half_sin
    return 1.0 - twice * half_sin, twice * half_cos


def spin(value, step, size, sign):
    real, imag = value
    step = step % size
    if step == 0:
        return value
    if 4 * step == size:
        return (-imag, real) if sign > 0 else (imag, -real)
    if 2 * step == size:
        return (-real, -imag)
    if 4 * step == 3 * size:
        return (imag, -real) if sign > 0 else (-imag, real)
    cos = math.cos(2 * math.pi * step / size)
    sin = sign * math.sin(2 * math.pi * step / size)
    if 8 * step % size == 0 and abs(abs(cos) - abs(sin)) < 1e-9:
        root = abs(cos)
        real, imag = real * root, imag * root
        cs = 1 if cos > 0 else -1
        ss = 1 if sin > 0 else -1
        a = real if cs > 0 else -real
        new_real = a - imag if ss > 0 else a + imag
        b = imag if cs > 0 else -imag
        new_imag = b + real if ss > 0 else b - real
        return new_real, new_imag
    return real * cos - imag * sin, real * sin + imag * cos


def small_dft(values, sign):
    size = len(values)
    if size == 1:
        return values
    even = small_dft(values[0::2], sign)
    odd = small_dft(values[1::2], sign)
    low, high = [], []
    for k in range(size // 2):
        turned = spin(odd[k], k, size, sign)
        low.append((even[k][0] + turned[0], even[k][1] + turned[1]))
        high.append((even[k][0] - turned[0], even[k][1] - turned[1]))
    return low + high


def dft32(load, store, mid_ref, sign):
    for b in range(8):
        out = small_dft([load(8 * a + b) for a in range(4)], sign)
        for p in range(4):
            real, imag = spin(out[p], b * p, 32, sign)
            mid_ref[8 * p + b, 0] = real
            mid_ref[8 * p + b, 1] = imag
    for p in range(4):
        out = small_dft([(mid_ref[8 * p + b, 0], mid_ref[8 * p + b, 1]) for b in range(8)], sign)
        for s in range(8):
            store(p + 4 * s, out[s])


def split(value):
    high = value.astype(BF16)
    return high, (value - high.astype(F32)).astype(BF16)


def dot(left, right):
    return jnp.dot(left, right, preferred_element_type=F32)


def row_block(step):
    return pl.ds(pl.multiple_of(step * BLOCK, BLOCK), BLOCK)


def tile(index):
    return slice(index * INNER, (index + 1) * INNER)


def sort_kernel(depth_ref, target_ref, out_ref, turned_ref):
    for k in range(OUTER):
        turned_ref[tile(k), :] = target_ref[:, tile(k)].T
    for j in range(OUTER):
        out_ref[j, :INNER] = turned_ref[pl.ds(j, INNER, stride=OUTER), :].T
        out_ref[j, INNER:] = jnp.full((NOTE, INNER), depth_ref[0].astype(F32))


def rows_kernel(
    length, place_ref, phase_ref, targets_hbm, out_hbm, wave_hbm, tw_ref, tall_ref, dft_ref, *refs
):
    sent = refs[:-13]
    high_ref, low_ref, mid_ref, sh_ref, sl_ref, out_ref, wave_ref, row_ref, col_ref, note_ref, stage_ref, sem, send_sem = refs[-13:]
    layers = len(sent) + 1
    group = targets_hbm.shape[0] // layers
    layer = place_ref[0]

    note = pltpu.make_async_copy(targets_hbm.at[layer * group, pl.ds(INNER, NOTE)], note_ref, sem.at[2])
    note.start()
    stage = pltpu.make_async_copy(targets_hbm.at[:, pl.ds(0, INNER)], stage_ref, sem.at[3])
    stage.start()
    sends = [
        pltpu.make_async_copy(
            stage_ref.at[pl.ds(lax.rem(layer + k, layers) * group, group)],
            sent[k - 1],
            send_sem.at[k - 1],
        )
        for k in range(1, layers)
    ]
    note.wait()
    modulus = 2 * length
    weight = inverse_odd(
        ((note_ref[0:1, :].astype(jnp.int32) + 8) * (length // 64) + 1) & (modulus - 1), modulus
    )

    def index(shape, axis):
        return lax.broadcasted_iota(jnp.int32, shape, axis)

    def waves(steps, size):
        return unit_wave(steps.astype(F32) * (-1.0 / size))

    flat = (OUTER, INNER)
    tw_ref[0], tw_ref[1] = waves((index(flat, 0) * index(flat, 1) * weight) & (length - 1), length)
    tall = (INNER, OUTER)
    tall_ref[0], tall_ref[1] = waves(
        (index(tall, 0) * index(tall, 1) * weight[:, :OUTER]) & (length - 1), length
    )
    square = (INNER, INNER)
    steps = (index(square, 0) * index(square, 1)) & (INNER - 1)
    cos, sin = waves((steps * (weight & (INNER - 1))) & (INNER - 1), INNER)
    cos, sin = cos * (1.0 / math.sqrt(length)), sin * (1.0 / math.sqrt(length))
    dft_ref[:INNER, :INNER], dft_ref[:INNER, INNER:] = cos, sin
    dft_ref[INNER:, :INNER], dft_ref[INNER:, INNER:] = -sin, cos
    high_ref[...], low_ref[...] = split(dft_ref[...])

    def chirp(pixel):
        return ((((pixel * pixel) & (modulus - 1)) * weight) & (modulus - 1)).astype(F32) * (1.0 / modulus)

    col_ref[...] = chirp(index(flat, 0) * INNER + index(flat, 1))
    local = index(square, 0)
    inside = local & (BLOCK - 1)
    row_ref[...] = chirp((local - inside) * (length // layers // BLOCK) + place_ref[1] + inside)

    def save_wave(step):
        rows = row_block(step)
        return pltpu.make_async_copy(wave_ref.at[:, rows, :], wave_hbm.at[:, rows, :], sem.at[0])

    def save_out(step):
        group = pl.ds(step * 4, 4)
        return pltpu.make_async_copy(out_ref.at[group], out_hbm.at[group], sem.at[1])

    def block(step, carry):
        rows = row_block(step)
        row_turn = row_ref[rows, :]

        def load(k):
            turns = phase_ref[rows, tile(k)] * (0.5 / math.pi) + (row_turn + col_ref[k : k + 1, :])
            cos, sin = unit_wave(turns)
            wave_ref[0, rows, tile(k)] = cos
            wave_ref[1, rows, tile(k)] = sin
            return cos, sin

        def store(k, value):
            cos, sin = tw_ref[0, k : k + 1, :], tw_ref[1, k : k + 1, :]
            real, imag = value
            for part, side in ((real * cos - imag * sin, 0), (real * sin + imag * cos, 1)):
                high, low = split(part)
                sh_ref[k, rows, tile(side)] = high
                sl_ref[k, rows, tile(side)] = low

        dft32(load, store, mid_ref, -1)
        save_wave(step).start()
        return carry

    lax.fori_loop(0, INNER // BLOCK, block, 0)
    stage.wait()
    for send in sends:
        send.start()

    def multiply(step, carry):
        group = pl.ds(step * 4, 4)
        high = sh_ref[group].reshape(4 * INNER, 2 * INNER)
        low = sl_ref[group].reshape(4 * INNER, 2 * INNER)
        out = dot(
            jnp.concatenate([high, low, high], axis=1),
            jnp.concatenate([high_ref[...], high_ref[...], low_ref[...]], axis=0),
        )
        out = out.reshape(4, INNER, 2 * INNER)
        out_ref[group, 0] = out[:, :, :INNER]
        out_ref[group, 1] = out[:, :, INNER:]
        save_out(step).start()
        return carry

    lax.fori_loop(0, OUTER // 4, multiply, 0)
    pltpu.make_async_copy(wave_ref, wave_hbm, sem.at[0]).wait()
    pltpu.make_async_copy(out_ref, out_hbm, sem.at[1]).wait()
    for send in sends:
        send.wait()


def columns_kernel(
    scale, layer_ref, tw_ref, there_ref, in_hbm, *refs
):
    pieces_hbm, refs = refs[: len(refs) - 11], refs[len(refs) - 11 :]
    out_ref, there_both, home_both, mid_ref, sh_ref, sl_ref, back_ref, target_ref, in_ref, pieces_ref, sem = refs
    layers = len(pieces_hbm)
    run = INNER // layers

    def fetch(step):
        group = pl.ds(step * 4, 4)
        return pltpu.make_async_copy(in_hbm.at[group], in_ref.at[group], sem.at[step])

    def fetch_piece(k):
        return pltpu.make_async_copy(pieces_hbm[k], pieces_ref.at[k], sem.at[INNER // BLOCK + k])

    for step in range(INNER // BLOCK):
        fetch(step).start()
    for k in range(layers):
        fetch_piece(k).start()

    for both, matrix in ((there_both, transposed(there_ref)), (home_both, there_ref[...])):
        high, low = split(matrix)
        both[...] = jnp.concatenate([high, low, high], axis=1)

    def forward(step, carry):
        rows = row_block(step)
        fetch(step).wait()

        def load(k):
            return tuple(in_ref[step * 4 + k % 4, side, tile_rows(k // 4), :] for side in (0, 1))

        def store(k, value):
            cos, sin = tw_ref[0, rows, k : k + 1], tw_ref[1, rows, k : k + 1]
            real, imag = value
            for part, side in ((real * cos - imag * sin, 0), (real * sin + imag * cos, 1)):
                high, low = split(part)
                sh_ref[k, side, rows, :] = high
                sl_ref[k, side, rows, :] = low

        dft32(load, store, mid_ref, -1)
        return carry

    lax.fori_loop(0, INNER // BLOCK, forward, 0)

    for k in range(layers):
        fetch_piece(k).wait()
        start = lax.rem(layer_ref[0] + (layers - k), layers) * run
        spot = pl.ds(pl.multiple_of(start, run), run)
        for u0 in range(OUTER):
            target_ref[u0, spot, :] = pieces_ref[k, pl.ds(u0, run, stride=OUTER), :]

    def wide(ref, first):
        return jnp.concatenate([ref[first + k].reshape(2 * INNER, INNER) for k in range(WIDE)], axis=1)

    def product(table_ref, high, low):
        return dot(table_ref[...], jnp.concatenate([high, high, low], axis=0))

    def multiply(step, carry):
        first = step * WIDE
        field = product(there_both, wide(sh_ref, first), wide(sl_ref, first))
        real, imag = field[:INNER], field[INNER:]
        target = jnp.concatenate([target_ref[first + k] for k in range(WIDE)], axis=1)
        residual = scale * (real * real + imag * imag - target)
        back = product(home_both, *split(jnp.concatenate([residual * real, residual * imag], axis=0)))
        for k in range(WIDE):
            back_ref[first + k] = back[:, tile(k)].reshape(2, INNER, INNER)
        return carry

    lax.fori_loop(0, OUTER // WIDE, multiply, 0)

    def backward(step, carry):
        rows = row_block(step)

        def load(k):
            cos, sin = tw_ref[0, rows, k : k + 1], tw_ref[1, rows, k : k + 1]
            real, imag = back_ref[k, 0, rows, :], back_ref[k, 1, rows, :]
            return real * cos + imag * sin, imag * cos - real * sin

        def store(k, value):
            for side in (0, 1):
                out_ref[step * 4 + k % 4, side, tile_rows(k // 4), :] = value[side]

        dft32(load, store, mid_ref, 1)
        return carry

    lax.fori_loop(0, INNER // BLOCK, backward, 0)


def transposed(ref):
    return jnp.concatenate(
        [
            jnp.concatenate([ref[:INNER, :INNER], ref[INNER:, :INNER]], axis=1),
            jnp.concatenate([ref[:INNER, INNER:], ref[INNER:, INNER:]], axis=1),
        ],
        axis=0,
    )


def tile_rows(index):
    return slice(index * BLOCK, (index + 1) * BLOCK)


def gradient_kernel(in_ref, wave_ref, tw_ref, dft_ref, out_ref, high_ref, low_ref, mid_ref, back_ref):
    high_ref[...], low_ref[...] = split(transposed(dft_ref))

    def multiply(step, carry):
        group = pl.ds(step * 4, 4)
        both = jnp.concatenate([in_ref[group, 0], in_ref[group, 1]], axis=-1).reshape(4 * INNER, 2 * INNER)
        high, low = split(both)
        out = dot(
            jnp.concatenate([high, low, high], axis=1),
            jnp.concatenate([high_ref[...], high_ref[...], low_ref[...]], axis=0),
        )
        back_ref[group] = out.reshape(4, INNER, 2 * INNER)
        return carry

    lax.fori_loop(0, OUTER // 4, multiply, 0)

    def block(step, carry):
        rows = row_block(step)

        def load(k):
            cos, sin = tw_ref[0, k : k + 1, :], tw_ref[1, k : k + 1, :]
            real, imag = back_ref[k, rows, tile(0)], back_ref[k, rows, tile(1)]
            return real * cos + imag * sin, imag * cos - real * sin

        def store(k, value):
            out_ref[rows, tile(k)] = value[1] * wave_ref[0, rows, tile(k)] - value[0] * wave_ref[1, rows, tile(k)]

        dft32(load, store, mid_ref, 1)
        return carry

    lax.fori_loop(0, INNER // BLOCK, block, 0)


def call(kernel, out_shapes, scratch, *args, direct=(), limit=28, held=0):
    return pl.pallas_call(
        kernel,
        out_shape=[jax.ShapeDtypeStruct(shape, F32) for shape in out_shapes],
        in_specs=[
            pl.BlockSpec(
                memory_space=pltpu.SMEM if arg.dtype == jnp.int32 else pl.ANY if k >= len(args) - held else pltpu.VMEM
            )
            for k, arg in enumerate(args)
        ],
        out_specs=[pl.BlockSpec(memory_space=pltpu.HBM if k in direct else pltpu.VMEM) for k in range(len(out_shapes))],
        scratch_shapes=[pltpu.VMEM(*item) if isinstance(item, tuple) else item for item in scratch],
        compiler_params=pltpu.CompilerParams(vmem_limit_bytes=limit * 2**20),
    )(*args)


def inverse_odd(value, modulus):
    result = value
    for _ in range(4):
        result = (result * ((2 - value * result) & (modulus - 1))) & (modulus - 1)
    return result


def on_device(phase, depths, targets):
    rows_dev, length = phase.shape
    planes = lax.axis_size("xl") * lax.axis_size("y")
    layers = lax.axis_size("z")
    place = lax.axis_index("xl") * lax.axis_size("y") + lax.axis_index("y")
    slab_size = math.prod(lax.axis_size(axis) for axis in SLAB)
    share = rows_dev // planes
    mine = lax.dynamic_slice_in_dim(phase, place * share, share, 0)
    mine, targets = lax.optimization_barrier((mine, targets))
    rows_phase = lax.all_gather(mine, "z", axis=0, tiled=True)

    (sorted_targets,) = call(
        sort_kernel,
        [(slab_size, rows_dev + NOTE, INNER)],
        [((length, rows_dev), F32)],
        depths,
        targets[0],
        limit=60,
    )
    sorted_targets = lax.all_to_all(sorted_targets, SLAB, 0, 0, tiled=True)
    layer = lax.axis_index("z")
    group = slab_size // layers
    layer_index = layer.astype(jnp.int32)
    first_row = (lax.axis_index("xh") * lax.axis_size("c") + lax.axis_index("c")) * rows_dev + place * share

    mid = ((OUTER, 2, BLOCK, INNER), F32)
    matrix = ((2 * INNER, 2 * INNER), BF16)
    chunks = (slab_size, 2, layers * share, INNER)
    spectrum, wave, twiddle, tall_twiddle, there, *sent = call(
        functools.partial(rows_kernel, length),
        [
            chunks,
            (2, layers * share, length),
            (2, OUTER, INNER),
            (2, INNER, OUTER),
            (2 * INNER, 2 * INNER),
        ]
        + [(group, rows_dev, INNER)] * (layers - 1),
        [
            matrix,
            matrix,
            mid,
            ((OUTER, INNER, 2 * INNER), BF16),
            ((OUTER, INNER, 2 * INNER), BF16),
            (chunks, F32),
            ((2, layers * share, length), F32),
            ((INNER, INNER), F32),
            ((OUTER, INNER), F32),
            ((NOTE, INNER), F32),
            ((slab_size, rows_dev, INNER), F32),
            pltpu.SemaphoreType.DMA((4,)),
            pltpu.SemaphoreType.DMA((layers - 1,)),
        ],
        jnp.stack([layer_index, first_row.astype(jnp.int32)]),
        rows_phase,
        sorted_targets,
        held=1,
        direct=(0, 1) + tuple(range(5, 4 + layers)),
        limit=60,
    )
    own = lax.dynamic_slice(sorted_targets, (layer * group, 0, 0), (group, rows_dev, INNER))
    pieces = [own] + [
        lax.ppermute(piece, "z", [(i, (i + k) % layers) for i in range(layers)]) for k, piece in enumerate(sent, 1)
    ]
    pieces = [piece.reshape(group * rows_dev, INNER) for piece in pieces]
    spectrum = lax.all_to_all(spectrum, SLAB, 0, 0, tiled=True)
    (spectrum,) = call(
        lambda *refs: columns_kernel(4.0 / planes, *refs),
        [chunks],
        [
            ((2 * INNER, 6 * INNER), BF16),
            ((2 * INNER, 6 * INNER), BF16),
            mid,
            ((OUTER, 2, INNER, INNER), BF16),
            ((OUTER, 2, INNER, INNER), BF16),
            ((OUTER, 2, INNER, INNER), F32),
            ((OUTER, INNER, INNER), F32),
            (chunks, F32),
            ((layers, group * rows_dev, INNER), F32),
            pltpu.SemaphoreType.DMA((INNER // BLOCK + layers,)),
        ],
        layer_index[None],
        tall_twiddle,
        there,
        spectrum,
        *pieces,
        held=1 + layers,
    )
    spectrum = lax.all_to_all(spectrum, SLAB, 0, 0, tiled=True)
    (part,) = call(
        gradient_kernel,
        [(layers * share, length)],
        [matrix, matrix, mid, ((OUTER, INNER, 2 * INNER), F32)],
        spectrum,
        wave,
        twiddle,
        there,
    )
    part = lax.psum_scatter(part, "z", scatter_dimension=0, tiled=True)
    part = jnp.broadcast_to(part[None], (planes, share, length))
    return lax.all_to_all(part, ("xl", "y"), 0, 0, tiled=True).reshape(rows_dev, length)


def solution(mesh):
    fine = Mesh(mesh.devices.reshape(2, 4, 8, 2, 2), ("xl", "y", "z", "xh", "c"))
    rows = ("z", "xh", "c")
    placed = (P(rows, None), P(("xl", "y")), P(("xl", "y"), rows, None))
    return jax.shard_map(on_device, mesh=fine, in_specs=placed, out_specs=P(rows, None), check_vma=False)
```

```python
import functools
import math

import jax
import jax.numpy as jnp
import numpy as np
from jax import lax
from jax.experimental import pallas as pl
from jax.experimental.pallas import tpu as pltpu
from jax.sharding import Mesh
from jax.sharding import PartitionSpec as P

SLAB = ("xl", "y", "xh", "c")
OUTER = 32
INNER = 128
BLOCK = 16
WIDE = 16
NOTE = 8
F32 = jnp.float32
BF16 = jnp.bfloat16


def fit(function, count, odd):
    points = np.cos(np.pi * (np.arange(400) + 0.5) / 400) * 0.5
    powers = np.stack([points ** (2 * k + odd) for k in range(count)], axis=1)
    return [float(c) for c in np.linalg.lstsq(powers, function(np.pi * points), rcond=None)[0]]


SIN_TERMS = fit(np.sin, 6, 1)
COS_TERMS = fit(np.cos, 6, 0)


def horner(terms, square):
    total = jnp.full_like(square, terms[-1])
    for term in terms[-2::-1]:
        total = total * square + term
    return total


def unit_wave(turns):
    turns = turns - jnp.round(turns)
    square = turns * turns
    half_sin = turns * horner(SIN_TERMS, square)
    half_cos = horner(COS_TERMS, square)
    twice = half_sin + half_sin
    return 1.0 - twice * half_sin, twice * half_cos


def spin(value, step, size, sign):
    real, imag = value
    step = step % size
    if step == 0:
        return value
    if 4 * step == size:
        return (-imag, real) if sign > 0 else (imag, -real)
    if 2 * step == size:
        return (-real, -imag)
    if 4 * step == 3 * size:
        return (imag, -real) if sign > 0 else (-imag, real)
    cos = math.cos(2 * math.pi * step / size)
    sin = sign * math.sin(2 * math.pi * step / size)
    if 8 * step % size == 0 and abs(abs(cos) - abs(sin)) < 1e-9:
        root = abs(cos)
        real, imag = real * root, imag * root
        cs = 1 if cos > 0 else -1
        ss = 1 if sin > 0 else -1
        a = real if cs > 0 else -real
        new_real = a - imag if ss > 0 else a + imag
        b = imag if cs > 0 else -imag
        new_imag = b + real if ss > 0 else b - real
        return new_real, new_imag
    return real * cos - imag * sin, real * sin + imag * cos


def small_dft(values, sign):
    size = len(values)
    if size == 1:
        return values
    even = small_dft(values[0::2], sign)
    odd = small_dft(values[1::2], sign)
    low, high = [], []
    for k in range(size // 2):
        turned = spin(odd[k], k, size, sign)
        low.append((even[k][0] + turned[0], even[k][1] + turned[1]))
        high.append((even[k][0] - turned[0], even[k][1] - turned[1]))
    return low + high


def dft32(load, store, mid_ref, sign):
    for b in range(8):
        out = small_dft([load(8 * a + b) for a in range(4)], sign)
        for p in range(4):
            real, imag = spin(out[p], b * p, 32, sign)
            mid_ref[8 * p + b, 0] = real
            mid_ref[8 * p + b, 1] = imag
    for p in range(4):
        out = small_dft([(mid_ref[8 * p + b, 0], mid_ref[8 * p + b, 1]) for b in range(8)], sign)
        for s in range(8):
            store(p + 4 * s, out[s])


def split(value):
    high = value.astype(BF16)
    return high, (value - high.astype(F32)).astype(BF16)


def dot(left, right):
    return jnp.dot(left, right, preferred_element_type=F32)


def row_block(step):
    return pl.ds(pl.multiple_of(step * BLOCK, BLOCK), BLOCK)


def tile(index):
    return slice(index * INNER, (index + 1) * INNER)


def sort_kernel(depth_ref, target_ref, out_ref, turned_ref):
    for k in range(OUTER):
        turned_ref[tile(k), :] = target_ref[:, tile(k)].T
    for j in range(OUTER):
        out_ref[j, :INNER] = turned_ref[pl.ds(j, INNER, stride=OUTER), :].T
        out_ref[j, INNER:] = jnp.full((NOTE, INNER), depth_ref[0].astype(F32))


def rows_kernel(
    length, place_ref, phase_ref, targets_hbm, out_hbm, wave_hbm, tw_ref, tall_ref, dft_ref, *refs
):
    sent = refs[:-13]
    high_ref, low_ref, mid_ref, sh_ref, sl_ref, out_ref, wave_ref, row_ref, col_ref, note_ref, stage_ref, sem, send_sem = refs[-13:]
    layers = len(sent) + 1
    group = targets_hbm.shape[0] // layers
    layer = place_ref[0]

    note = pltpu.make_async_copy(targets_hbm.at[layer * group, pl.ds(INNER, NOTE)], note_ref, sem.at[2])
    note.start()
    stage = pltpu.make_async_copy(targets_hbm.at[:, pl.ds(0, INNER)], stage_ref, sem.at[3])
    stage.start()
    sends = [
        pltpu.make_async_copy(
            stage_ref.at[pl.ds(lax.rem(layer + k, layers) * group, group)],
            sent[k - 1],
            send_sem.at[k - 1],
        )
        for k in range(1, layers)
    ]
    note.wait()
    modulus = 2 * length
    weight = inverse_odd(
        ((note_ref[0:1, :].astype(jnp.int32) + 8) * (length // 64) + 1) & (modulus - 1), modulus
    )

    def index(shape, axis):
        return lax.broadcasted_iota(jnp.int32, shape, axis)

    def waves(steps, size):
        return unit_wave(steps.astype(F32) * (-1.0 / size))

    flat = (OUTER, INNER)
    tw_ref[0], tw_ref[1] = waves((index(flat, 0) * index(flat, 1) * weight) & (length - 1), length)
    tall = (INNER, OUTER)
    tall_ref[0], tall_ref[1] = waves(
        (index(tall, 0) * index(tall, 1) * weight[:, :OUTER]) & (length - 1), length
    )
    square = (INNER, INNER)
    steps = (index(square, 0) * index(square, 1)) & (INNER - 1)
    cos, sin = waves((steps * (weight & (INNER - 1))) & (INNER - 1), INNER)
    cos, sin = cos * (1.0 / math.sqrt(length)), sin * (1.0 / math.sqrt(length))
    dft_ref[:INNER, :INNER], dft_ref[:INNER, INNER:] = cos, sin
    dft_ref[INNER:, :INNER], dft_ref[INNER:, INNER:] = -sin, cos
    high_ref[...], low_ref[...] = split(dft_ref[...])

    def chirp(pixel):
        return ((((pixel * pixel) & (modulus - 1)) * weight) & (modulus - 1)).astype(F32) * (1.0 / modulus)

    col_ref[...] = chirp(index(flat, 0) * INNER + index(flat, 1))
    local = index(square, 0)
    inside = local & (BLOCK - 1)
    row_ref[...] = chirp((local - inside) * (length // layers // BLOCK) + place_ref[1] + inside)

    def save_wave(step):
        rows = row_block(step)
        return pltpu.make_async_copy(wave_ref.at[:, rows, :], wave_hbm.at[:, rows, :], sem.at[0])

    def save_out(step):
        group = pl.ds(step * 4, 4)
        return pltpu.make_async_copy(out_ref.at[group], out_hbm.at[group], sem.at[1])

    def block(step, carry):
        rows = row_block(step)
        row_turn = row_ref[rows, :]

        def load(k):
            turns = phase_ref[rows, tile(k)] * (0.5 / math.pi) + (row_turn + col_ref[k : k + 1, :])
            cos, sin = unit_wave(turns)
            wave_ref[0, rows, tile(k)] = cos
            wave_ref[1, rows, tile(k)] = sin
            return cos, sin

        def store(k, value):
            cos, sin = tw_ref[0, k : k + 1, :], tw_ref[1, k : k + 1, :]
            real, imag = value
            for part, side in ((real * cos - imag * sin, 0), (real * sin + imag * cos, 1)):
                high, low = split(part)
                sh_ref[k, rows, tile(side)] = high
                sl_ref[k, rows, tile(side)] = low

        dft32(load, store, mid_ref, -1)
        save_wave(step).start()
        return carry

    lax.fori_loop(0, INNER // BLOCK, block, 0)
    stage.wait()
    for send in sends:
        send.start()

    def multiply(step, carry):
        group = pl.ds(step * 4, 4)
        high = sh_ref[group].reshape(4 * INNER, 2 * INNER)
        low = sl_ref[group].reshape(4 * INNER, 2 * INNER)
        out = dot(
            jnp.concatenate([high, low, high], axis=1),
            jnp.concatenate([high_ref[...], high_ref[...], low_ref[...]], axis=0),
        )
        out = out.reshape(4, INNER, 2 * INNER)
        out_ref[group, 0] = out[:, :, :INNER]
        out_ref[group, 1] = out[:, :, INNER:]
        save_out(step).start()
        return carry

    lax.fori_loop(0, OUTER // 4, multiply, 0)
    pltpu.make_async_copy(wave_ref, wave_hbm, sem.at[0]).wait()
    pltpu.make_async_copy(out_ref, out_hbm, sem.at[1]).wait()
    for send in sends:
        send.wait()


def columns_kernel(
    scale, layer_ref, tw_ref, there_ref, in_hbm, *refs
):
    pieces_hbm, refs = refs[: len(refs) - 11], refs[len(refs) - 11 :]
    out_ref, there_both, home_both, mid_ref, sh_ref, sl_ref, back_ref, target_ref, in_ref, pieces_ref, sem = refs
    layers = len(pieces_hbm)
    run = INNER // layers

    def fetch(step):
        group = pl.ds(step * 4, 4)
        return pltpu.make_async_copy(in_hbm.at[group], in_ref.at[group], sem.at[step])

    def fetch_piece(k):
        return pltpu.make_async_copy(pieces_hbm[k], pieces_ref.at[k], sem.at[INNER // BLOCK + k])

    for step in range(INNER // BLOCK):
        fetch(step).start()
    for k in range(layers):
        fetch_piece(k).start()

    for both, matrix in ((there_both, transposed(there_ref)), (home_both, there_ref[...])):
        high, low = split(matrix)
        both[...] = jnp.concatenate([high, low, high], axis=1)

    def forward(step, carry):
        rows = row_block(step)
        fetch(step).wait()

        def load(k):
            return tuple(in_ref[step * 4 + k % 4, side, tile_rows(k // 4), :] for side in (0, 1))

        def store(k, value):
            cos, sin = tw_ref[0, rows, k : k + 1], tw_ref[1, rows, k : k + 1]
            real, imag = value
            for part, side in ((real * cos - imag * sin, 0), (real * sin + imag * cos, 1)):
                high, low = split(part)
                sh_ref[k, side, rows, :] = high
                sl_ref[k, side, rows, :] = low

        dft32(load, store, mid_ref, -1)
        return carry

    lax.fori_loop(0, INNER // BLOCK, forward, 0)

    for k in range(layers):
        fetch_piece(k).wait()
        start = lax.rem(layer_ref[0] + (layers - k), layers) * run
        spot = pl.ds(pl.multiple_of(start, run), run)
        for u0 in range(OUTER):
            target_ref[u0, spot, :] = pieces_ref[k, pl.ds(u0, run, stride=OUTER), :]

    def wide(ref, first):
        return jnp.concatenate([ref[first + k].reshape(2 * INNER, INNER) for k in range(WIDE)], axis=1)

    def product(table_ref, high, low):
        return dot(table_ref[...], jnp.concatenate([high, high, low], axis=0))

    def multiply(step, carry):
        first = step * WIDE
        field = product(there_both, wide(sh_ref, first), wide(sl_ref, first))
        real, imag = field[:INNER], field[INNER:]
        target = jnp.concatenate([target_ref[first + k] for k in range(WIDE)], axis=1)
        residual = scale * (real * real + imag * imag - target)
        back = product(home_both, *split(jnp.concatenate([residual * real, residual * imag], axis=0)))
        for k in range(WIDE):
            back_ref[first + k] = back[:, tile(k)].reshape(2, INNER, INNER)
        return carry

    lax.fori_loop(0, OUTER // WIDE, multiply, 0)

    def backward(step, carry):
        rows = row_block(step)

        def load(k):
            cos, sin = tw_ref[0, rows, k : k + 1], tw_ref[1, rows, k : k + 1]
            real, imag = back_ref[k, 0, rows, :], back_ref[k, 1, rows, :]
            return real * cos + imag * sin, imag * cos - real * sin

        def store(k, value):
            for side in (0, 1):
                out_ref[step * 4 + k % 4, side, tile_rows(k // 4), :] = value[side]

        dft32(load, store, mid_ref, 1)
        return carry

    lax.fori_loop(0, INNER // BLOCK, backward, 0)


def transposed(ref):
    return jnp.concatenate(
        [
            jnp.concatenate([ref[:INNER, :INNER], ref[INNER:, :INNER]], axis=1),
            jnp.concatenate([ref[:INNER, INNER:], ref[INNER:, INNER:]], axis=1),
        ],
        axis=0,
    )


def tile_rows(index):
    return slice(index * BLOCK, (index + 1) * BLOCK)


def gradient_kernel(in_ref, wave_ref, tw_ref, dft_ref, out_ref, high_ref, low_ref, mid_ref, back_ref):
    high_ref[...], low_ref[...] = split(transposed(dft_ref))

    def multiply(step, carry):
        group = pl.ds(step * 8, 8)
        both = jnp.concatenate([in_ref[group, 0], in_ref[group, 1]], axis=-1).reshape(8 * INNER, 2 * INNER)
        high, low = split(both)
        out = dot(
            jnp.concatenate([high, low, high], axis=1),
            jnp.concatenate([high_ref[...], high_ref[...], low_ref[...]], axis=0),
        )
        back_ref[group] = out.reshape(8, INNER, 2 * INNER)
        return carry

    lax.fori_loop(0, OUTER // 8, multiply, 0)

    def block(step, carry):
        rows = row_block(step)

        def load(k):
            cos, sin = tw_ref[0, k : k + 1, :], tw_ref[1, k : k + 1, :]
            real, imag = back_ref[k, rows, tile(0)], back_ref[k, rows, tile(1)]
            return real * cos + imag * sin, imag * cos - real * sin

        def store(k, value):
            out_ref[rows, tile(k)] = value[1] * wave_ref[0, rows, tile(k)] - value[0] * wave_ref[1, rows, tile(k)]

        dft32(load, store, mid_ref, 1)
        return carry

    lax.fori_loop(0, INNER // BLOCK, block, 0)


def call(kernel, out_shapes, scratch, *args, direct=(), limit=28, held=0):
    return pl.pallas_call(
        kernel,
        out_shape=[jax.ShapeDtypeStruct(shape, F32) for shape in out_shapes],
        in_specs=[
            pl.BlockSpec(
                memory_space=pltpu.SMEM if arg.dtype == jnp.int32 else pl.ANY if k >= len(args) - held else pltpu.VMEM
            )
            for k, arg in enumerate(args)
        ],
        out_specs=[pl.BlockSpec(memory_space=pltpu.HBM if k in direct else pltpu.VMEM) for k in range(len(out_shapes))],
        scratch_shapes=[pltpu.VMEM(*item) if isinstance(item, tuple) else item for item in scratch],
        compiler_params=pltpu.CompilerParams(vmem_limit_bytes=limit * 2**20),
    )(*args)


def inverse_odd(value, modulus):
    result = value
    for _ in range(4):
        result = (result * ((2 - value * result) & (modulus - 1))) & (modulus - 1)
    return result


def on_device(phase, depths, targets):
    rows_dev, length = phase.shape
    planes = lax.axis_size("xl") * lax.axis_size("y")
    layers = lax.axis_size("z")
    place = lax.axis_index("xl") * lax.axis_size("y") + lax.axis_index("y")
    slab_size = math.prod(lax.axis_size(axis) for axis in SLAB)
    share = rows_dev // planes
    mine = lax.dynamic_slice_in_dim(phase, place * share, share, 0)
    mine, targets = lax.optimization_barrier((mine, targets))
    rows_phase = lax.all_gather(mine, "z", axis=0, tiled=True)

    (sorted_targets,) = call(
        sort_kernel,
        [(slab_size, rows_dev + NOTE, INNER)],
        [((length, rows_dev), F32)],
        depths,
        targets[0],
        limit=60,
    )
    sorted_targets = lax.all_to_all(sorted_targets, SLAB, 0, 0, tiled=True)
    layer = lax.axis_index("z")
    group = slab_size // layers
    layer_index = layer.astype(jnp.int32)
    first_row = (lax.axis_index("xh") * lax.axis_size("c") + lax.axis_index("c")) * rows_dev + place * share

    mid = ((OUTER, 2, BLOCK, INNER), F32)
    matrix = ((2 * INNER, 2 * INNER), BF16)
    chunks = (slab_size, 2, layers * share, INNER)
    spectrum, wave, twiddle, tall_twiddle, there, *sent = call(
        functools.partial(rows_kernel, length),
        [
            chunks,
            (2, layers * share, length),
            (2, OUTER, INNER),
            (2, INNER, OUTER),
            (2 * INNER, 2 * INNER),
        ]
        + [(group, rows_dev, INNER)] * (layers - 1),
        [
            matrix,
            matrix,
            mid,
            ((OUTER, INNER, 2 * INNER), BF16),
            ((OUTER, INNER, 2 * INNER), BF16),
            (chunks, F32),
            ((2, layers * share, length), F32),
            ((INNER, INNER), F32),
            ((OUTER, INNER), F32),
            ((NOTE, INNER), F32),
            ((slab_size, rows_dev, INNER), F32),
            pltpu.SemaphoreType.DMA((4,)),
            pltpu.SemaphoreType.DMA((layers - 1,)),
        ],
        jnp.stack([layer_index, first_row.astype(jnp.int32)]),
        rows_phase,
        sorted_targets,
        held=1,
        direct=(0, 1) + tuple(range(5, 4 + layers)),
        limit=60,
    )
    own = lax.dynamic_slice(sorted_targets, (layer * group, 0, 0), (group, rows_dev, INNER))
    pieces = [own] + [
        lax.ppermute(piece, "z", [(i, (i + k) % layers) for i in range(layers)]) for k, piece in enumerate(sent, 1)
    ]
    pieces = [piece.reshape(group * rows_dev, INNER) for piece in pieces]
    spectrum = lax.all_to_all(spectrum, SLAB, 0, 0, tiled=True)
    (spectrum,) = call(
        lambda *refs: columns_kernel(4.0 / planes, *refs),
        [chunks],
        [
            ((2 * INNER, 6 * INNER), BF16),
            ((2 * INNER, 6 * INNER), BF16),
            mid,
            ((OUTER, 2, INNER, INNER), BF16),
            ((OUTER, 2, INNER, INNER), BF16),
            ((OUTER, 2, INNER, INNER), F32),
            ((OUTER, INNER, INNER), F32),
            (chunks, F32),
            ((layers, group * rows_dev, INNER), F32),
            pltpu.SemaphoreType.DMA((INNER // BLOCK + layers,)),
        ],
        layer_index[None],
        tall_twiddle,
        there,
        spectrum,
        *pieces,
        held=1 + layers,
    )
    spectrum = lax.all_to_all(spectrum, SLAB, 0, 0, tiled=True)
    (part,) = call(
        gradient_kernel,
        [(layers * share, length)],
        [matrix, matrix, mid, ((OUTER, INNER, 2 * INNER), F32)],
        spectrum,
        wave,
        twiddle,
        there,
    )
    part = lax.psum_scatter(part, "z", scatter_dimension=0, tiled=True)
    part = jnp.broadcast_to(part[None], (planes, share, length))
    return lax.all_to_all(part, ("xl", "y"), 0, 0, tiled=True).reshape(rows_dev, length)


def solution(mesh):
    fine = Mesh(mesh.devices.reshape(2, 4, 8, 2, 2), ("xl", "y", "z", "xh", "c"))
    rows = ("z", "xh", "c")
    placed = (P(rows, None), P(("xl", "y")), P(("xl", "y"), rows, None))
    return jax.shard_map(on_device, mesh=fine, in_specs=placed, out_specs=P(rows, None), check_vma=False)
```
